128 devices in a mesh: day: 4 (over x), chan: 32 (over y, z, core).
Axes of the slice: x: 4, y: 4, z: 4, core: 2. Of those that a mesh axis runs over, the one named last changes fastest.
Arguments:
- strain_raw: bfloat16 [8, 4096, 1024], P('day', 'chan'), may hold values from -320 to 320, as said below
- pair_dist: int32 [32, 3], P('chan'), may hold values from -1 to 4, as said below
Outputs:
- stack: float32 [96, 129, 128, 128], P('chan', None, 'day')
The draws below stay inside these ranges and needn't reach their ends.
Inputs may be any that keep to these rules, and one draw needn't show every extreme that they name: `pair_dist`: each owner's live slots come first and hold distinct distances with c + distance below 32; every owner has at least one live slot and owner 0 has all 3 live, one of them at distance 4. `strain_raw`: channels differ in scale and offset.
All inputs are finite; a program needn't handle non-finite values.
Results may differ from the reference program's by a relative error of at most 0.0039.
Values may be sent and summed in bfloat16 or wider, within the bound.
No kernel may reach another device: no remote copies, remote signals or barrier semaphores. Data moves between devices by JAX's collectives and lax.ppermute only.
A program may use at most 256 MiB of HBM per device.

```python
import math
import jax
import jax.numpy as jnp
from jax import lax

BW = 128
SAMPLES = 1024
MAXLAG = 64
REACH = 4
TILES_DEV = 3
LAGS = 129
DAYS = 8
NBLK = 32
CHANNELS = 4096


def draw_strain_raw(key, part):
    key = jax.random.fold_in(key, 11)
    key_scale = jax.random.fold_in(key, 0)
    key_noise = jax.random.fold_in(key, 1)
    key_offset = jax.random.fold_in(key, 3)
    scale = jnp.exp(jax.random.uniform(key_scale, (DAYS, CHANNELS, 1), jnp.float32, 0.0, math.log(10.0)))
    base = jnp.clip(jax.random.normal(key_noise, (DAYS, CHANNELS, SAMPLES), jnp.float32), -6.0, 6.0)
    offset = jnp.clip(jax.random.normal(key_offset, (DAYS, CHANNELS, 1), jnp.float32), -3.0, 3.0)
    return jnp.clip((base + offset) * scale, -320.0, 320.0).astype(jnp.bfloat16)


def draw_pair_dist(key, part):
    key = jax.random.fold_in(key, 23)
    key_order, key_count = jax.random.split(key, 2)
    owners = jnp.arange(NBLK, dtype=jnp.int32)[:, None]
    dists = jnp.arange(REACH + 1, dtype=jnp.int32)[None, :]
    avail = jnp.minimum(REACH, NBLK - 1 - owners) + 1
    scores = jax.random.randint(key_order, (NBLK, REACH + 1), 0, 1000, dtype=jnp.int32) * (REACH + 1) + dists
    scores = jnp.where(dists < avail, scores, 10000000)
    scores = scores.at[0, REACH].set(-1)
    order = jnp.argsort(scores, axis=1).astype(jnp.int32)
    count = jax.random.randint(key_count, (NBLK, 1), 1, TILES_DEV + 1, dtype=jnp.int32)
    count = jnp.minimum(count, avail)
    count = count.at[0, 0].set(TILES_DEV)
    slots = jnp.arange(TILES_DEV, dtype=jnp.int32)[None, :]
    return jnp.where(slots < count, order[:, :TILES_DEV], -1).astype(jnp.int32)


def setup_inputs(seed: int = 0) -> dict:
    key_list = jax.random.split(jax.random.key(seed), 3)
    strain_raw = draw_strain_raw(jax.random.fold_in(key_list[2], 71), 0)
    pair_dist = draw_pair_dist(jax.random.fold_in(key_list[2], 71), 0)
    return dict(strain_raw=strain_raw, pair_dist=pair_dist)


def whiten_all(strain_raw):
    values = strain_raw.astype(jnp.float32)
    centred = values - lax.optimization_barrier(jnp.mean(values, axis=-1, keepdims=True))
    spread = lax.optimization_barrier(jnp.mean(centred * centred, axis=-1, keepdims=True))
    return (centred * lax.rsqrt(spread + 1e-06)).astype(jnp.bfloat16)

def reference(strain_raw, pair_dist):
    whitened = whiten_all(strain_raw)
    blocks = whitened.reshape(DAYS, NBLK, BW, SAMPLES).transpose(1, 0, 2, 3)
    padded = jnp.pad(blocks, ((0, 0), (0, 0), (0, 0), (MAXLAG, MAXLAG)))
    owners = (jnp.arange(NBLK * TILES_DEV) // TILES_DEV).astype(jnp.int32)
    dists = pair_dist.reshape(-1).astype(jnp.int32)
    norm = 1.0 / jnp.sqrt(jnp.float32(SAMPLES * DAYS))

    def one_pair(item):
        owner, dist = item
        first = lax.dynamic_index_in_dim(blocks, owner, 0, keepdims=False).astype(jnp.float32)
        partner = lax.dynamic_index_in_dim(padded, owner + jnp.maximum(dist, 0), 0, keepdims=False).astype(jnp.float32)

        def one_lag(lag_index):
            shifted = lax.dynamic_slice_in_dim(partner, lag_index, SAMPLES, 2)
            return jnp.einsum('dis,djs->ij', first, shifted)
        tile = lax.map(one_lag, jnp.arange(LAGS, dtype=jnp.int32)) * norm
        return jnp.where(dist >= 0, tile, jnp.zeros_like(tile))
    return lax.map(one_pair, (owners, dists))
```

```python
import functools
import jax
import jax.numpy as jnp
from jax import lax
from jax.experimental import pallas as pl
from jax.experimental.pallas import tpu as pltpu
from jax.sharding import PartitionSpec as P

BW = 128
SAMPLES = 1024
MAXLAG = 64
REACH = 4
TILES_DEV = 3
LAGS = 2 * MAXLAG + 1
SHIFTS = MAXLAG + 1
GROUP = 13
GROUPS = SHIFTS // GROUP
BF = jnp.bfloat16


def whiten_kernel(raw_ref, out_ref):
    values = raw_ref[...].astype(jnp.float32)
    centred = values - jnp.mean(values, axis=-1, keepdims=True)
    spread = jnp.mean(centred * centred, axis=-1, keepdims=True)
    out_ref[...] = (centred * lax.rsqrt(spread + 1e-06)).astype(BF)


def whiten(strain_raw):
    days, chans, samples = strain_raw.shape
    spec = pl.BlockSpec((days, 32, samples), lambda i: (0, i, 0))
    return pl.pallas_call(
        whiten_kernel,
        grid=(chans // 32,),
        in_specs=[spec],
        out_specs=spec,
        out_shape=jax.ShapeDtypeStruct(strain_raw.shape, BF),
        cost_estimate=pl.CostEstimate(
            flops=8 * strain_raw.size, bytes_accessed=4 * strain_raw.size, transcendentals=0
        ),
        name="whiten",
    )(strain_raw)


def correlate_kernel(sets, reach, first, norm, win, *refs):
    per_set = 1 + len(reach)
    blocks = [refs[s * per_set : (s + 1) * per_set] for s in range(sets)]
    refs = refs[sets * per_set :]
    if not first:
        refs = refs[1:]
    out_ref, araw, braw, left, right, acc, *rest = refs
    shifted, (sem_a, sem_b, sem_in, sem_out) = rest[:GROUPS], rest[GROUPS:]
    days = araw.shape[1]
    rows = araw.shape[2]
    row0 = pl.multiple_of(win[0] * rows, rows)

    def live(k):
        dist = win[1 + k]
        if first and len(reach) == REACH + 1:
            return dist >= 0
        hit = dist == reach[0]
        for e in reach[1:]:
            hit = jnp.logical_or(hit, dist == e)
        return hit

    lives = [live(k) for k in range(TILES_DEV)]
    any_live = jnp.logical_or(jnp.logical_or(lives[0], lives[1]), lives[2])

    def copy_in(k):
        return pltpu.make_async_copy(out_ref.at[k], acc.at[k], sem_in.at[k])

    def copy_out(k):
        return pltpu.make_async_copy(acc.at[k], out_ref.at[k], sem_out.at[k])

    def copy_left(s):
        return pltpu.make_async_copy(
            blocks[s][0].at[:, pl.ds(row0, rows), :], araw.at[s], sem_a.at[s]
        )

    @pl.when(any_live)
    def _():
        for s in range(sets):
            copy_left(s).start()
            for k in range(TILES_DEV):
                for n, e in enumerate(reach):

                    @pl.when(win[1 + k] == e)
                    def _():
                        pltpu.make_async_copy(
                            blocks[s][1 + n], braw.at[s, k], sem_b.at[s, k]
                        ).start()

        if not first:
            for k in range(TILES_DEV):

                @pl.when(lives[k])
                def _():
                    copy_in(k).start()

        if not first:
            for k in range(TILES_DEV):

                @pl.when(lives[k])
                def _():
                    copy_in(k).wait()

        gap = jnp.zeros((rows, MAXLAG), BF)
        gap_b = jnp.zeros((BW, MAXLAG), BF)

        def make_shift(g):
            for i in range(GROUP):
                shift = g * GROUP + i
                value = left[...]
                if shift:
                    value = pltpu.roll(value, shift, 1)
                shifted[g][i * rows : (i + 1) * rows, :] = value

        def one_set(s, carry):
            pltpu.make_async_copy(
                blocks[0][0].at[:, pl.ds(0, rows), :], araw.at[s], sem_a.at[s]
            ).wait()
            left[...] = jnp.concatenate(
                [p for d in range(days) for p in (araw[s, d], gap)], 1
            )

            def one_slot(k, seen):
                dist = win[1 + k]
                hit = dist == reach[0]
                for e in reach[1:]:
                    hit = jnp.logical_or(hit, dist == e)

                def work(with_shift):
                    pltpu.make_async_copy(
                        blocks[0][1], braw.at[s, k], sem_b.at[s, k]
                    ).wait()
                    right[0:BW, :] = jnp.concatenate(
                        [p for d in range(days) for p in (gap_b, braw[s, k, d])], 1
                    )
                    right[BW : 2 * BW, :] = jnp.concatenate(
                        [p for d in range(days) for p in (braw[s, k, d], gap_b)], 1
                    )
                    if with_shift:
                        make_shift(0)
                    for g in range(GROUPS):
                        if with_shift and g + 1 < GROUPS:
                            make_shift(g + 1)
                        part = lax.dot_general(
                            shifted[g][...],
                            right[...],
                            (((1,), (1,)), ((), ())),
                            preferred_element_type=jnp.float32,
                        )
                        part = part * norm
                        low = part[:, :BW].reshape(GROUP, rows, BW)
                        high = part[:, BW:].reshape(GROUP, rows, BW)
                        lo_at = pl.ds(g * GROUP, GROUP)
                        hi_at = pl.ds(MAXLAG + g * GROUP, GROUP)
                        if g == GROUPS - 1:
                            lo_at = pl.ds(g * GROUP, GROUP - 1)
                            low = low[: GROUP - 1]
                        if sets == 1 and first:
                            acc[k, lo_at] = low
                            acc[k, hi_at] = high
                        else:
                            acc[k, lo_at] += low
                            acc[k, hi_at] += high

                @pl.when(jnp.logical_and(hit, seen == 0))
                def _():
                    work(True)

                @pl.when(jnp.logical_and(hit, seen != 0))
                def _():
                    work(False)

                @pl.when(jnp.logical_and(hit, s == sets - 1))
                def _():
                    copy_out(k).start()

                return seen + hit.astype(jnp.int32)

            lax.fori_loop(0, TILES_DEV, one_slot, jnp.int32(0))
            return carry

        lax.fori_loop(0, sets, one_set, 0)

    if first:
        for k in range(TILES_DEV):

            @pl.when(jnp.logical_not(lives[k]))
            def _():
                acc[k] = jnp.zeros(acc.shape[1:], jnp.float32)
                copy_out(k).start()

        for k in range(TILES_DEV):
            copy_out(k).wait()
    else:
        for k in range(TILES_DEV):

            @pl.when(lives[k])
            def _():
                copy_out(k).wait()


def correlate(sets, reach, scalars, total, rows, norm, name):
    days = sets[0][0].shape[0]
    count = len(sets)
    span = days * (SAMPLES + MAXLAG)
    operands = []
    for own, partners in sets:
        operands += [own] + [partners[e] for e in reach]
    first = total is None
    aliases = {}
    if not first:
        aliases = {1 + len(operands): 0}
        operands.append(total)
    tile = (TILES_DEV, LAGS, rows, BW)
    any_spec = pl.BlockSpec(memory_space=pl.ANY)
    flops = 2 * 2 * count * TILES_DEV * SHIFTS * rows * BW * span * 2 // 2
    return pl.pallas_call(
        functools.partial(correlate_kernel, count, reach, first, norm),
        grid_spec=pltpu.PrefetchScalarGridSpec(
            num_scalar_prefetch=1,
            grid=(1,),
            in_specs=[any_spec] * len(operands),
            out_specs=any_spec,
            scratch_shapes=[
                pltpu.VMEM((count, days, rows, SAMPLES), BF),
                pltpu.VMEM((count, TILES_DEV, days, BW, SAMPLES), BF),
                pltpu.VMEM((rows, span), BF),
                pltpu.VMEM((2 * BW, span), BF),
                pltpu.VMEM(tile, jnp.float32),
            ]
            + [pltpu.VMEM((GROUP * rows, span), BF)] * GROUPS
            + [
                pltpu.SemaphoreType.DMA((count,)),
                pltpu.SemaphoreType.DMA((count, TILES_DEV)),
                pltpu.SemaphoreType.DMA((TILES_DEV,)),
                pltpu.SemaphoreType.DMA((TILES_DEV,)),
            ],
        ),
        out_shape=jax.ShapeDtypeStruct(tile, jnp.float32),
        input_output_aliases=aliases,
        compiler_params=pltpu.CompilerParams(vmem_limit_bytes=40 << 20),
        cost_estimate=pl.CostEstimate(
            flops=flops, bytes_accessed=8 << 20, transcendentals=0
        ),
        name=name,
    )(scalars, *operands)


def moved(array, axis, by):
    devices = lax.axis_size(axis)
    if axis == "day":
        pairs = [(i, (i + by) % devices) for i in range(devices)]
    else:
        pairs = [(i, i + by) for i in range(devices) if 0 <= i + by < devices]
    return lax.ppermute(array, axis, pairs)


def swapped(array):
    devices = lax.axis_size("chan")
    return lax.ppermute(array, "chan", [(i, i ^ 1) for i in range(devices)])


def local(strain_raw, pair_dist):
    day = lax.axis_index("day")
    even = lax.axis_index("chan") % 2 == 0
    rows = BW // lax.axis_size("day")
    total_days = strain_raw.shape[0] * lax.axis_size("day")
    norm = float((SAMPLES * total_days) ** -0.5)
    scalars = jnp.concatenate([day.astype(jnp.int32)[None], pair_dist[0].astype(jnp.int32)])

    own = whiten(strain_raw)
    z2 = moved(own, "chan", -2)
    own_p, own_m = moved(own, "day", 1), moved(own, "day", -1)
    z4 = moved(own, "chan", -4)
    own_2 = moved(own, "day", 2)
    z2_p, z2_m = moved(z2, "day", 1), moved(z2, "day", -1)
    z2_2, z4_2 = moved(own_2, "chan", -2), moved(own_2, "chan", -4)
    z4_p, z4_m = moved(z4, "day", 1), moved(z4, "day", -1)

    def with_pair(mine, two, four):
        odd_ones = swapped(jnp.where(even, two, mine))
        even_ones = swapped(jnp.where(even, four, two))
        return mine, {0: mine, 1: odd_ones, 2: two, 3: even_ones, 4: four}

    reach = tuple(range(REACH + 1))
    tiles = correlate([with_pair(own, z2, z4)], reach, scalars, None, rows, norm, "near_days")
    others = [
        with_pair(own_p, z2_p, z4_p),
        with_pair(own_m, z2_m, z4_m),
        with_pair(own_2, z2_2, z4_2),
    ]
    return correlate(others, reach, scalars, tiles, rows, norm, "far_days")


def solution(mesh):
    placed = (P("day", "chan", None), P("chan", None))
    return jax.shard_map(
        local, mesh=mesh, in_specs=placed, out_specs=P("chan", None, "day", None), check_vma=False
    )
```

```python
import functools
import jax
import jax.numpy as jnp
from jax import lax
from jax.experimental import pallas as pl
from jax.experimental.pallas import tpu as pltpu
from jax.sharding import PartitionSpec as P

BW = 128
SAMPLES = 1024
MAXLAG = 64
REACH = 4
TILES_DEV = 3
LAGS = 2 * MAXLAG + 1
SHIFTS = MAXLAG + 1
GROUP = 13
GROUPS = SHIFTS // GROUP
BF = jnp.bfloat16


def whiten_kernel(raw_ref, out_ref):
    values = raw_ref[...].astype(jnp.float32)
    centred = values - jnp.mean(values, axis=-1, keepdims=True)
    spread = jnp.mean(centred * centred, axis=-1, keepdims=True)
    out_ref[...] = (centred * lax.rsqrt(spread + 1e-06)).astype(BF)


def whiten(strain_raw):
    days, chans, samples = strain_raw.shape
    spec = pl.BlockSpec((days, 32, samples), lambda i: (0, i, 0))
    return pl.pallas_call(
        whiten_kernel,
        grid=(chans // 32,),
        in_specs=[spec],
        out_specs=spec,
        out_shape=jax.ShapeDtypeStruct(strain_raw.shape, BF),
        cost_estimate=pl.CostEstimate(
            flops=8 * strain_raw.size, bytes_accessed=4 * strain_raw.size, transcendentals=0
        ),
        name="whiten",
    )(strain_raw)


def correlate_kernel(places, operands, reach, first, norm, win, *refs):
    sets = len(places)
    arrays, refs = refs[:operands], refs[operands:]
    if not first:
        refs = refs[1:]
    out_ref, araw, braw, left, right, acc, *rest = refs
    shifted, (sem_a, sem_b, sem_in, sem_out) = rest[:GROUPS], rest[GROUPS:]
    days = araw.shape[1]
    rows = araw.shape[2]
    row0 = pl.multiple_of(win[0] * rows, rows)

    def live(k):
        dist = win[1 + k]
        if first and len(reach) == REACH + 1:
            return dist >= 0
        hit = dist == reach[0]
        for e in reach[1:]:
            hit = jnp.logical_or(hit, dist == e)
        return hit

    lives = [live(k) for k in range(TILES_DEV)]
    any_live = jnp.logical_or(jnp.logical_or(lives[0], lives[1]), lives[2])

    def copy_in(k):
        return pltpu.make_async_copy(out_ref.at[k], acc.at[k], sem_in.at[k])

    def copy_out(k):
        return pltpu.make_async_copy(acc.at[k], out_ref.at[k], sem_out.at[k])

    def copy_left(s):
        array, start = places[s][0]
        return pltpu.make_async_copy(
            arrays[array].at[pl.ds(start, days), pl.ds(row0, rows), :], araw.at[s], sem_a.at[s]
        )

    def copy_right(s, k, n):
        array, start = places[s][1 + n]
        return pltpu.make_async_copy(
            arrays[array].at[pl.ds(start, days)], braw.at[s, k], sem_b.at[s, k]
        )

    @pl.when(any_live)
    def _():
        for s in range(sets):
            copy_left(s).start()
            for k in range(TILES_DEV):
                for n, e in enumerate(reach):

                    @pl.when(win[1 + k] == e)
                    def _():
                        copy_right(s, k, n).start()

        if not first:
            for k in range(TILES_DEV):

                @pl.when(lives[k])
                def _():
                    copy_in(k).start()

        if not first:
            for k in range(TILES_DEV):

                @pl.when(lives[k])
                def _():
                    copy_in(k).wait()

        gap = jnp.zeros((rows, MAXLAG), BF)
        gap_b = jnp.zeros((BW, MAXLAG), BF)

        def make_shift(g):
            for i in range(GROUP):
                shift = g * GROUP + i
                value = left[...]
                if shift:
                    value = pltpu.roll(value, shift, 1)
                shifted[g][i * rows : (i + 1) * rows, :] = value

        def one_set(s, carry):
            pltpu.make_async_copy(araw.at[s], araw.at[s], sem_a.at[s]).wait()
            left[...] = jnp.concatenate(
                [p for d in range(days) for p in (araw[s, d], gap)], 1
            )

            def one_slot(k, seen):
                dist = win[1 + k]
                hit = dist == reach[0]
                for e in reach[1:]:
                    hit = jnp.logical_or(hit, dist == e)

                def work(with_shift):
                    pltpu.make_async_copy(
                        braw.at[s, k], braw.at[s, k], sem_b.at[s, k]
                    ).wait()
                    right[0:BW, :] = jnp.concatenate(
                        [p for d in range(days) for p in (gap_b, braw[s, k, d])], 1
                    )
                    right[BW : 2 * BW, :] = jnp.concatenate(
                        [p for d in range(days) for p in (braw[s, k, d], gap_b)], 1
                    )
                    if with_shift:
                        make_shift(0)
                    for g in range(GROUPS):
                        if with_shift and g + 1 < GROUPS:
                            make_shift(g + 1)
                        part = lax.dot_general(
                            shifted[g][...],
                            right[...],
                            (((1,), (1,)), ((), ())),
                            preferred_element_type=jnp.float32,
                        )
                        part = part * norm
                        low = part[:, :BW].reshape(GROUP, rows, BW)
                        high = part[:, BW:].reshape(GROUP, rows, BW)
                        lo_at = pl.ds(g * GROUP, GROUP)
                        hi_at = pl.ds(MAXLAG + g * GROUP, GROUP)
                        if g == GROUPS - 1:
                            lo_at = pl.ds(g * GROUP, GROUP - 1)
                            low = low[: GROUP - 1]
                        if sets == 1 and first:
                            acc[k, lo_at] = low
                            acc[k, hi_at] = high
                        else:
                            acc[k, lo_at] += low
                            acc[k, hi_at] += high

                @pl.when(jnp.logical_and(hit, seen == 0))
                def _():
                    work(True)

                @pl.when(jnp.logical_and(hit, seen != 0))
                def _():
                    work(False)

                @pl.when(jnp.logical_and(hit, s == sets - 1))
                def _():
                    copy_out(k).start()

                return seen + hit.astype(jnp.int32)

            lax.fori_loop(0, TILES_DEV, one_slot, jnp.int32(0))
            return carry

        lax.fori_loop(0, sets, one_set, 0)

    if first:
        for k in range(TILES_DEV):

            @pl.when(jnp.logical_not(lives[k]))
            def _():
                acc[k] = jnp.zeros(acc.shape[1:], jnp.float32)
                copy_out(k).start()

        for k in range(TILES_DEV):
            copy_out(k).wait()
    else:
        for k in range(TILES_DEV):

            @pl.when(lives[k])
            def _():
                copy_out(k).wait()


def correlate(sets, reach, scalars, total, rows, norm, name):
    days = 2
    count = len(sets)
    span = days * (SAMPLES + MAXLAG)
    operands = []

    def place(block):
        array, start = block
        for i, other in enumerate(operands):
            if other is array:
                return i, start
        operands.append(array)
        return len(operands) - 1, start

    places = [
        [place(own)] + [place(partners[e]) for e in reach] for own, partners in sets
    ]
    arrays = len(operands)
    first = total is None
    aliases = {}
    if not first:
        aliases = {1 + len(operands): 0}
        operands.append(total)
    tile = (TILES_DEV, LAGS, rows, BW)
    any_spec = pl.BlockSpec(memory_space=pl.ANY)
    flops = 4 * count * len(reach) * SHIFTS * rows * BW * span
    return pl.pallas_call(
        functools.partial(correlate_kernel, places, arrays, reach, first, norm),
        grid_spec=pltpu.PrefetchScalarGridSpec(
            num_scalar_prefetch=1,
            grid=(1,),
            in_specs=[any_spec] * len(operands),
            out_specs=any_spec,
            scratch_shapes=[
                pltpu.VMEM((count, days, rows, SAMPLES), BF),
                pltpu.VMEM((count, TILES_DEV, days, BW, SAMPLES), BF),
                pltpu.VMEM((rows, span), BF),
                pltpu.VMEM((2 * BW, span), BF),
                pltpu.VMEM(tile, jnp.float32),
            ]
            + [pltpu.VMEM((GROUP * rows, span), BF)] * GROUPS
            + [
                pltpu.SemaphoreType.DMA((count,)),
                pltpu.SemaphoreType.DMA((count, TILES_DEV)),
                pltpu.SemaphoreType.DMA((TILES_DEV,)),
                pltpu.SemaphoreType.DMA((TILES_DEV,)),
            ],
        ),
        out_shape=jax.ShapeDtypeStruct(tile, jnp.float32),
        input_output_aliases=aliases,
        compiler_params=pltpu.CompilerParams(vmem_limit_bytes=40 << 20),
        cost_estimate=pl.CostEstimate(
            flops=flops, bytes_accessed=8 << 20, transcendentals=0
        ),
        name=name,
    )(scalars, *operands)


def moved(array, axis, by):
    devices = lax.axis_size(axis)
    if axis == "day":
        pairs = [(i, (i + by) % devices) for i in range(devices)]
    else:
        pairs = [(i, i + by) for i in range(devices) if 0 <= i + by < devices]
    return lax.ppermute(array, axis, pairs)


def swapped(array):
    devices = lax.axis_size("chan")
    return lax.ppermute(array, "chan", [(i, i ^ 1) for i in range(devices)])


def local(strain_raw, pair_dist):
    day = lax.axis_index("day")
    even = lax.axis_index("chan") % 2 == 0
    rows = BW // lax.axis_size("day")
    total_days = strain_raw.shape[0] * lax.axis_size("day")
    norm = float((SAMPLES * total_days) ** -0.5)
    scalars = jnp.concatenate([day.astype(jnp.int32)[None], pair_dist[0].astype(jnp.int32)])

    own = whiten(strain_raw)
    tie = lax.optimization_barrier

    def pick(even_ones, odd_ones):
        return jnp.where(even, jnp.concatenate(even_ones), jnp.concatenate(odd_ones))

    z2, z4 = moved(own, "chan", -2), moved(own, "chan", -4)
    own_p, own_m, own_2 = (moved(own, "day", by) for by in (1, -1, 2))
    z2, z4, own_p, own_m, own_2 = tie((z2, z4, own_p, own_m, own_2))

    z2_p, z2_m = moved(z2, "day", 1), moved(z2, "day", -1)
    z2_2 = moved(own_2, "chan", -2)
    pair = swapped(pick((z2, z4), (own, z2)))
    near = ((own, 0), {0: (own, 0), 1: (pair, 0), 2: (z2, 0), 3: (pair, 2), 4: (z4, 0)})
    tiles = correlate([near], (0, 1, 2, 3, 4), scalars, None, rows, norm, "near_days")
    z2_p, z2_m, z2_2, z4, own_2, tiles = tie((z2_p, z2_m, z2_2, z4, own_2, tiles))

    z4_p, z4_m = moved(z4, "day", 1), moved(z4, "day", -1)
    z4_2 = moved(own_2, "chan", -4)
    odd = swapped(pick((z2_p, z2_m, z2_2), (own_p, own_m, own_2)))
    mine = (own_p, own_m, own_2)
    two = (z2_p, z2_m, z2_2)
    sets = [
        ((mine[i], 0), {0: (mine[i], 0), 1: (odd, 2 * i), 2: (two[i], 0)}) for i in range(3)
    ]
    tiles = correlate(sets, (0, 1, 2), scalars, tiles, rows, norm, "far_days_low")
    z4_p, z4_m, z4_2, tiles = tie((z4_p, z4_m, z4_2, tiles))

    four = (z4_p, z4_m, z4_2)
    far = swapped(pick(four, two))
    sets = [((mine[i], 0), {3: (far, 2 * i), 4: (four[i], 0)}) for i in range(3)]
    return correlate(sets, (3, 4), scalars, tiles, rows, norm, "far_days_high")


def solution(mesh):
    placed = (P("day", "chan", None), P("chan", None))
    return jax.shard_map(
        local, mesh=mesh, in_specs=placed, out_specs=P("chan", None, "day", None), check_vma=False
    )
```

```python
import functools
import jax
import jax.numpy as jnp
from jax import lax
from jax.experimental import pallas as pl
from jax.experimental.pallas import tpu as pltpu
from jax.sharding import PartitionSpec as P

BW = 128
SAMPLES = 1024
MAXLAG = 64
REACH = 4
TILES_DEV = 3
LAGS = 2 * MAXLAG + 1
SHIFTS = MAXLAG + 1
GROUP = 13
GROUPS = SHIFTS // GROUP
BF = jnp.bfloat16


def whiten_kernel(raw_ref, out_ref):
    values = raw_ref[...].astype(jnp.float32)
    centred = values - jnp.mean(values, axis=-1, keepdims=True)
    spread = jnp.mean(centred * centred, axis=-1, keepdims=True)
    out_ref[...] = (centred * lax.rsqrt(spread + 1e-06)).astype(BF)


def whiten(strain_raw):
    return pl.pallas_call(
        whiten_kernel,
        in_specs=[pl.BlockSpec(memory_space=pltpu.VMEM)],
        out_specs=pl.BlockSpec(memory_space=pltpu.VMEM),
        out_shape=jax.ShapeDtypeStruct(strain_raw.shape, BF),
        cost_estimate=pl.CostEstimate(
            flops=8 * strain_raw.size, bytes_accessed=4 * strain_raw.size, transcendentals=0
        ),
        name="whiten",
    )(strain_raw)


def gather_kernel(moves, flag, *refs):
    arrays, outs, sems = refs[: moves[0]], refs[moves[0] : -1], refs[-1]
    for parity in (0, 1):

        @pl.when(flag[0] == parity)
        def _():
            copies = [
                pltpu.make_async_copy(
                    arrays[i].at[pl.ds(at, n)], outs[j].at[pl.ds(to, n)], sems.at[c]
                )
                for c, (i, at, j, to, n) in enumerate(moves[1 + parity])
            ]
            for copy in copies:
                copy.start()
            for copy in copies:
                copy.wait()


def gather(flag, arrays, counts, even, odd, name):
    any_spec = pl.BlockSpec(memory_space=pl.ANY)
    shape = arrays[0].shape[1:]
    return pl.pallas_call(
        functools.partial(gather_kernel, (len(arrays), even, odd)),
        grid_spec=pltpu.PrefetchScalarGridSpec(
            num_scalar_prefetch=1,
            grid=(1,),
            in_specs=[any_spec] * len(arrays),
            out_specs=[any_spec] * len(counts),
            scratch_shapes=[pltpu.SemaphoreType.DMA((max(len(even), len(odd)),))],
        ),
        out_shape=[jax.ShapeDtypeStruct((n,) + shape, BF) for n in counts],
        name=name,
    )(flag, *arrays)


def correlate_kernel(places, operands, reach, part, norm, win, *refs):
    sets = len(places)
    first = part == "all"
    arrays, refs = refs[:operands], refs[operands:]
    if not first:
        refs = refs[1:]
    out_ref, araw, braw, tiles, before, *refs = refs
    lefts, rights, refs = refs[:sets], refs[sets : 2 * sets], refs[2 * sets :]
    shifted, sums, sems = refs[: -sets - 3], refs[-sets - 3 : -4], refs[-4:]
    sem_a, sem_b, sem_in, sem_out = sems
    days, rows = araw.shape[1:3]
    slots = tiles.shape[0]
    row0 = pl.multiple_of(win[0] * rows, rows)

    lives, found = [], jnp.bool_(False)
    for k in range(TILES_DEV):
        dist = win[1 + k]
        plain = jnp.logical_and(dist >= 0, dist % 2 == 0)
        head = jnp.logical_and(plain, jnp.logical_not(found))
        found = jnp.logical_or(found, plain)
        if part == "all":
            lives.append(dist >= 0)
        elif part == "head":
            lives.append(head)
        else:
            lives.append(jnp.logical_and(dist >= 0, jnp.logical_not(head)))
    seats = [jnp.int32(0)]
    for k in range(TILES_DEV):
        seats.append(seats[-1] + lives[k].astype(jnp.int32))

    def copy_in(k, seat):
        return pltpu.make_async_copy(out_ref.at[k], before.at[seat], sem_in.at[seat])

    def copy_out(k, seat):
        return pltpu.make_async_copy(tiles.at[seat], out_ref.at[k], sem_out.at[seat])

    def copy_zero(k):
        return pltpu.make_async_copy(before, out_ref.at[k], sem_in.at[k])

    def copy_left(s):
        array, start = places[s][0]
        return pltpu.make_async_copy(
            arrays[array].at[pl.ds(start, days), pl.ds(row0, rows), :], araw.at[s], sem_a.at[s]
        )

    def copy_right(s, seat, n):
        array, start = places[s][1 + n]
        return pltpu.make_async_copy(
            arrays[array].at[pl.ds(start, days)], braw.at[seat, s], sem_b.at[seat, s]
        )

    @pl.when(seats[-1] > 0)
    def _():
        for s in range(sets):
            copy_left(s).start()
        for k in range(TILES_DEV):
            for n, e in enumerate(reach):

                @pl.when(jnp.logical_and(lives[k], win[1 + k] == e))
                def _():
                    for s in range(sets):
                        copy_right(s, seats[k], n).start()

            if not first:

                @pl.when(lives[k])
                def _():
                    copy_in(k, seats[k]).start()

        if first:
            before[...] = jnp.zeros(before.shape, jnp.float32)
            for k in range(TILES_DEV):
                pl.when(jnp.logical_not(lives[k]))(copy_zero(k).start)

        gap = jnp.zeros((rows, MAXLAG), BF)
        gap_b = jnp.zeros((BW, MAXLAG), BF)
        for s in range(sets):
            copy_left(s).wait()
            lefts[s][...] = jnp.concatenate(
                [p for d in range(days) for p in (araw[s, d], gap)], 1
            )

        def make_shift(s, g):
            for i in range(GROUP):
                shift = g * GROUP + i
                value = lefts[s][...]
                if shift:
                    value = pltpu.roll(value, shift, 1)
                shifted[(s * GROUPS + g) % len(shifted)][i * rows : (i + 1) * rows, :] = value

        def make_right(s, seat):
            rights[s][0:BW, :] = jnp.concatenate(
                [p for d in range(days) for p in (gap_b, braw[seat, s, d])], 1
            )
            rights[s][BW : 2 * BW, :] = jnp.concatenate(
                [p for d in range(days) for p in (braw[seat, s, d], gap_b)], 1
            )

        def one_slot(k, seat, with_shift):
            pltpu.make_async_copy(braw.at[seat, 0], braw.at[seat, 0], sem_b.at[seat, 0]).wait()
            make_right(0, seat)
            if with_shift:
                make_shift(0, 0)
            for s in range(sets):
                if s == 1:
                    for r in range(1, sets):
                        pltpu.make_async_copy(
                            braw.at[seat, r], braw.at[seat, r], sem_b.at[seat, r]
                        ).wait()
                        make_right(r, seat)
                    copy_in(k, seat).wait()
                for g in range(GROUPS):
                    if with_shift and g + 1 < GROUPS:
                        make_shift(s, g + 1)
                    elif with_shift and s + 1 < sets:
                        make_shift(s + 1, 0)
                    product = lax.dot_general(
                        shifted[(s * GROUPS + g) % len(shifted)][...],
                        rights[s][...],
                        (((1,), (1,)), ((), ())),
                        preferred_element_type=jnp.float32,
                    )
                    kept = GROUP - (g == GROUPS - 1)
                    for half, count, lag in (
                        (0, kept, g * GROUP),
                        (1, GROUP, MAXLAG + g * GROUP),
                    ):
                        value = product[:, half * BW : (half + 1) * BW].reshape(GROUP, rows, BW)
                        value = value[:count]
                        at = pl.ds(lag, count)
                        if s:
                            value = value + sums[s - 1][at]
                        if s + 1 < sets:
                            sums[s][at] = value
                        elif first:
                            tiles[seat, at] = value * norm
                        else:
                            tiles[seat, at] = value * norm + before[seat, at]
            copy_out(k, seat).start()

        def loop(k, seat):
            hit = lives[0]
            for n in range(1, TILES_DEV):
                hit = jnp.where(k == n, lives[n], hit)

            @pl.when(jnp.logical_and(hit, seat == 0))
            def _():
                one_slot(k, seat, True)

            if slots > 1:

                @pl.when(jnp.logical_and(hit, seat > 0))
                def _():
                    one_slot(k, seat, False)

            return seat + hit.astype(jnp.int32)

        lax.fori_loop(0, TILES_DEV, loop, jnp.int32(0))

    for k in range(TILES_DEV):
        pl.when(lives[k])(copy_out(k, seats[k]).wait)
        if first:
            pl.when(jnp.logical_not(lives[k]))(copy_zero(k).wait)


def correlate(sets, reach, part, slots, scalars, total, rows, norm, name):
    count = len(sets)
    days = 2
    span = days * (SAMPLES + MAXLAG)
    operands = []

    def place(block):
        array, start = block
        for i, other in enumerate(operands):
            if other is array:
                return i, start
        operands.append(array)
        return len(operands) - 1, start

    places = [
        [place(own)] + [place(partners[e]) for e in reach] for own, partners in sets
    ]
    arrays = len(operands)
    first = part == "all"
    aliases = {}
    if not first:
        aliases = {1 + len(operands): 0}
        operands.append(total)
    tile = (TILES_DEV, LAGS, rows, BW)
    any_spec = pl.BlockSpec(memory_space=pl.ANY)
    flops = 4 * count * slots * SHIFTS * rows * BW * span
    return pl.pallas_call(
        functools.partial(correlate_kernel, places, arrays, reach, part, norm),
        grid_spec=pltpu.PrefetchScalarGridSpec(
            num_scalar_prefetch=1,
            grid=(1,),
            in_specs=[any_spec] * len(operands),
            out_specs=any_spec,
            scratch_shapes=[
                pltpu.VMEM((count, days, rows, SAMPLES), BF),
                pltpu.VMEM((slots, count, days, BW, SAMPLES), BF),
                pltpu.VMEM((slots,) + tile[1:], jnp.float32),
                pltpu.VMEM(tile[1:] if first else (slots,) + tile[1:], jnp.float32),
            ]
            + [pltpu.VMEM((rows, span), BF)] * count
            + [pltpu.VMEM((2 * BW, span), BF)] * count
            + [pltpu.VMEM((GROUP * rows, span), BF)] * (GROUPS * count if slots > 1 else 2)
            + [pltpu.VMEM(tile[1:], jnp.float32)] * (count - 1)
            + [
                pltpu.SemaphoreType.DMA((count,)),
                pltpu.SemaphoreType.DMA((slots, count)),
                pltpu.SemaphoreType.DMA((TILES_DEV,)),
                pltpu.SemaphoreType.DMA((TILES_DEV,)),
            ],
        ),
        out_shape=jax.ShapeDtypeStruct(tile, jnp.float32),
        input_output_aliases=aliases,
        compiler_params=pltpu.CompilerParams(vmem_limit_bytes=(50 if count * slots > 3 else 30) << 20),
        cost_estimate=pl.CostEstimate(
            flops=flops, bytes_accessed=8 << 20, transcendentals=0
        ),
        name=name,
    )(scalars, *operands)


def moved(array, axis, by):
    devices = lax.axis_size(axis)
    if axis == "day":
        pairs = [(i, (i + by) % devices) for i in range(devices)]
    else:
        pairs = [(i, i + by) for i in range(devices) if 0 <= i + by < devices]
    return lax.ppermute(array, axis, pairs)


def swapped(array):
    devices = lax.axis_size("chan")
    return lax.ppermute(array, "chan", [(i, i ^ 1) for i in range(devices)])


def local(strain_raw, pair_dist):
    day = lax.axis_index("day")
    even = lax.axis_index("chan") % 2 == 0
    rows = BW // lax.axis_size("day")
    total_days = strain_raw.shape[0] * lax.axis_size("day")
    norm = float((SAMPLES * total_days) ** -0.5)
    scalars = jnp.concatenate([day.astype(jnp.int32)[None], pair_dist[0].astype(jnp.int32)])

    own = whiten(strain_raw)
    tie = lax.optimization_barrier
    parity = (lax.axis_index("chan") % 2).astype(jnp.int32)[None]

    z2, z4 = moved(own, "chan", -2), moved(own, "chan", -4)
    own_p, own_m, own_2 = (moved(own, "day", by) for by in (1, -1, 2))
    z2, z4, own_p, own_m, own_2 = tie((z2, z4, own_p, own_m, own_2))

    z2_2, z4_2 = moved(own_2, "chan", -2), moved(own_2, "chan", -4)
    both = [(1, 0, 0, 0, 2), (2, 0, 0, 2, 2)]
    zz, mine = gather(
        parity,
        (own, z2, z4),
        (4, 4),
        both + [(1, 0, 1, 0, 2), (2, 0, 1, 2, 2)],
        both + [(0, 0, 1, 0, 2), (1, 0, 1, 2, 2)],
        "pair_near",
    )
    zz_p, zz_m = moved(zz, "day", 1), moved(zz, "day", -1)
    pair = swapped(mine)
    near = ((own, 0), {0: (own, 0), 1: (pair, 0), 2: (z2, 0), 3: (pair, 2), 4: (z4, 0)})
    tiles = correlate([near], (0, 1, 2, 3, 4), "all", 3, scalars, None, rows, norm, "near_days")
    zz_p, zz_m, z2_2, z4_2, tiles = tie((zz_p, zz_m, z2_2, z4_2, tiles))

    (mine,) = gather(
        parity,
        (own_p, own_m, own_2, zz_p, zz_m, z2_2, z4_2),
        (12,),
        [(3, 0, 0, 0, 4), (4, 0, 0, 4, 4), (5, 0, 0, 8, 2), (6, 0, 0, 10, 2)],
        [
            (0, 0, 0, 0, 2),
            (3, 0, 0, 2, 2),
            (1, 0, 0, 4, 2),
            (4, 0, 0, 6, 2),
            (2, 0, 0, 8, 2),
            (5, 0, 0, 10, 2),
        ],
        "pair_far",
    )
    pair = swapped(mine)
    owns = (own_p, own_m, own_2)
    twos = ((zz_p, 0), (zz_m, 0), (z2_2, 0))
    fours = ((zz_p, 2), (zz_m, 2), (z4_2, 0))
    sets = [((owns[i], 0), {0: (owns[i], 0), 2: twos[i], 4: fours[i]}) for i in range(3)]
    tiles = correlate(sets, (0, 2, 4), "head", 1, scalars, tiles, rows, norm, "far_days_one")
    sets = [
        (
            (owns[i], 0),
            {
                0: (owns[i], 0),
                1: (pair, 4 * i),
                2: twos[i],
                3: (pair, 4 * i + 2),
                4: fours[i],
            },
        )
        for i in range(3)
    ]
    return correlate(sets, (0, 1, 2, 3, 4), "rest", 2, scalars, tiles, rows, norm, "far_days_rest")


def solution(mesh):
    placed = (P("day", "chan", None), P("chan", None))
    return jax.shard_map(
        local, mesh=mesh, in_specs=placed, out_specs=P("chan", None, "day", None), check_vma=False
    )
```

```python
import functools
import jax
import jax.numpy as jnp
from jax import lax
from jax.experimental import pallas as pl
from jax.experimental.pallas import tpu as pltpu
from jax.sharding import PartitionSpec as P

BW = 128
SAMPLES = 1024
MAXLAG = 64
REACH = 4
TILES_DEV = 3
LAGS = 2 * MAXLAG + 1
SHIFTS = MAXLAG + 1
GROUP = 13
GROUPS = SHIFTS // GROUP
BF = jnp.bfloat16


def whiten_kernel(raw_ref, out_ref):
    values = raw_ref[...].astype(jnp.float32)
    centred = values - jnp.mean(values, axis=-1, keepdims=True)
    spread = jnp.mean(centred * centred, axis=-1, keepdims=True)
    out_ref[...] = (centred * lax.rsqrt(spread + 1e-06)).astype(BF)


def whiten(strain_raw):
    return pl.pallas_call(
        whiten_kernel,
        in_specs=[pl.BlockSpec(memory_space=pltpu.VMEM)],
        out_specs=pl.BlockSpec(memory_space=pltpu.VMEM),
        out_shape=jax.ShapeDtypeStruct(strain_raw.shape, BF),
        cost_estimate=pl.CostEstimate(
            flops=8 * strain_raw.size, bytes_accessed=4 * strain_raw.size, transcendentals=0
        ),
        name="whiten",
    )(strain_raw)


def gather_kernel(moves, flag, *refs):
    arrays, outs, sems = refs[: moves[0]], refs[moves[0] : -1], refs[-1]
    for parity in (0, 1):

        @pl.when(flag[0] == parity)
        def _():
            copies = [
                pltpu.make_async_copy(
                    arrays[i].at[pl.ds(at, n)], outs[j].at[pl.ds(to, n)], sems.at[c]
                )
                for c, (i, at, j, to, n) in enumerate(moves[1 + parity])
            ]
            for copy in copies:
                copy.start()
            for copy in copies:
                copy.wait()


def gather(flag, arrays, counts, even, odd, name):
    vmem_spec = pl.BlockSpec(memory_space=pltpu.VMEM)
    any_spec = pl.BlockSpec(memory_space=pl.ANY)
    shape = arrays[0].shape[1:]
    return pl.pallas_call(
        functools.partial(gather_kernel, (len(arrays), even, odd)),
        in_specs=[pl.BlockSpec(memory_space=pltpu.SMEM)] + [any_spec] * len(arrays),
        out_specs=[vmem_spec] * len(counts),
        out_shape=[jax.ShapeDtypeStruct((n,) + shape, BF) for n in counts],
        scratch_shapes=[pltpu.SemaphoreType.DMA((max(len(even), len(odd)),))],
        compiler_params=pltpu.CompilerParams(vmem_limit_bytes=16 << 20),
        name=name,
    )(flag, *arrays)


def correlate_kernel(places, operands, part, norm, win, *refs):
    sets = len(places)
    first = part == "all"
    arrays, refs = refs[:operands], refs[operands:]
    if not first:
        refs = refs[1:]
    out_ref, araw, braw, tiles, before, *refs = refs
    lefts, rights, refs = refs[:sets], refs[sets : 2 * sets], refs[2 * sets :]
    shifted, sums, sems = refs[: 1 - sets - 4], refs[1 - sets - 4 : -4], refs[-4:]
    sem_a, sem_b, sem_in, sem_out = sems
    days, rows = araw.shape[1:3]
    slots = tiles.shape[0]
    row0 = pl.multiple_of(win[0] * rows, rows)

    lives, found = [], jnp.bool_(False)
    for k in range(TILES_DEV):
        dist = win[1 + k]
        plain = jnp.logical_and(dist >= 0, dist % 2 == 0)
        head = jnp.logical_and(plain, jnp.logical_not(found))
        found = jnp.logical_or(found, plain)
        if part == "all":
            lives.append(dist >= 0)
        elif part == "head":
            lives.append(head)
        else:
            lives.append(jnp.logical_and(dist >= 0, jnp.logical_not(head)))
    seats = [jnp.int32(0)]
    for k in range(TILES_DEV):
        seats.append(seats[-1] + lives[k].astype(jnp.int32))

    def copy_in(k, seat):
        return pltpu.make_async_copy(out_ref.at[k], before.at[seat], sem_in.at[seat])

    def copy_out(k, seat):
        return pltpu.make_async_copy(tiles.at[seat], out_ref.at[k], sem_out.at[seat])

    def copy_zero(k):
        return pltpu.make_async_copy(before, out_ref.at[k], sem_in.at[k])

    def copy_left(s):
        array, start = places[s][0]
        return pltpu.make_async_copy(
            arrays[array].at[pl.ds(start, days), pl.ds(row0, rows), :], araw.at[s], sem_a.at[s]
        )

    def copy_right(s, seat, n):
        array, start = places[s][1 + n]
        return pltpu.make_async_copy(
            arrays[array].at[pl.ds(start, days)], braw.at[seat, s], sem_b.at[seat, s]
        )

    @pl.when(seats[-1] > 0)
    def _():
        for s in range(sets):
            copy_left(s).start()
        for k in range(TILES_DEV):
            for e in range(0, REACH + 1, 2 if part == "head" else 1):

                @pl.when(jnp.logical_and(lives[k], win[1 + k] == e))
                def _():
                    for s in range(sets):
                        copy_right(s, seats[k], e).start()

            if not first:

                @pl.when(lives[k])
                def _():
                    copy_in(k, seats[k]).start()

        if first:
            before[...] = jnp.zeros(before.shape, jnp.float32)
            for k in range(TILES_DEV):
                pl.when(jnp.logical_not(lives[k]))(copy_zero(k).start)

        gap = jnp.zeros((rows, MAXLAG), BF)
        gap_b = jnp.zeros((BW, MAXLAG), BF)
        for s in range(sets):
            copy_left(s).wait()
            lefts[s][...] = jnp.concatenate(
                [p for d in range(days) for p in (araw[s, d], gap)], 1
            )

        def make_shift(s, g):
            for i in range(GROUP):
                shift = g * GROUP + i
                value = lefts[s][...]
                if shift:
                    value = pltpu.roll(value, shift, 1)
                shifted[(s * GROUPS + g) % len(shifted)][i * rows : (i + 1) * rows, :] = value

        def make_right(s, seat):
            rights[s][0:BW, :] = jnp.concatenate(
                [p for d in range(days) for p in (gap_b, braw[seat, s, d])], 1
            )
            rights[s][BW : 2 * BW, :] = jnp.concatenate(
                [p for d in range(days) for p in (braw[seat, s, d], gap_b)], 1
            )

        def work(seat, with_shift):
            for s in range(sets):
                copy_right(s, seat, 0).wait()
                make_right(s, seat)
            if not first:
                copy_in(0, seat).wait()
            if with_shift:
                make_shift(0, 0)
            for n in range(sets * GROUPS):
                s, g = divmod(n, GROUPS)
                if with_shift and n + 1 < sets * GROUPS:
                    make_shift(*divmod(n + 1, GROUPS))
                product = lax.dot_general(
                    shifted[n % len(shifted)][...],
                    rights[s][...],
                    (((1,), (1,)), ((), ())),
                    preferred_element_type=jnp.float32,
                )
                kept = GROUP - (g == GROUPS - 1)
                for half, count, lag in (
                    (0, kept, g * GROUP),
                    (1, GROUP, MAXLAG + g * GROUP),
                ):
                    value = product[:, half * BW : (half + 1) * BW]
                    value = value.reshape(GROUP, rows, BW)[:count]
                    at = pl.ds(lag, count)
                    if s:
                        value = value + sums[s - 1][at]
                    if s + 1 < sets:
                        sums[s][at] = value
                    elif first:
                        tiles[seat, at] = value * norm
                    else:
                        tiles[seat, at] = value * norm + before[seat, at]

        def loop(seat, carry):
            pl.when(seat == 0)(functools.partial(work, seat, True))
            if slots > 1:
                pl.when(seat > 0)(functools.partial(work, seat, False))
            for k in range(TILES_DEV):
                mine = jnp.logical_and(lives[k], seats[k] == seat)
                pl.when(mine)(copy_out(k, seat).start)
            return carry

        lax.fori_loop(0, seats[-1], loop, 0)

    for k in range(TILES_DEV):
        pl.when(lives[k])(copy_out(k, seats[k]).wait)
        if first:
            pl.when(jnp.logical_not(lives[k]))(copy_zero(k).wait)


def correlate(sets, part, slots, scalars, total, rows, norm, name):
    count = len(sets)
    days = 2
    span = days * (SAMPLES + MAXLAG)
    operands = []

    def place(block):
        array, start = block
        for i, other in enumerate(operands):
            if other is array:
                return i, start
        operands.append(array)
        return len(operands) - 1, start

    places = [
        [place(own)] + [place(partners.get(e, own)) for e in range(REACH + 1)] for own, partners in sets
    ]
    arrays = len(operands)
    first = part == "all"
    aliases = {}
    if not first:
        aliases = {1 + len(operands): 0}
        operands.append(total)
    tile = (TILES_DEV, LAGS, rows, BW)
    any_spec = pl.BlockSpec(memory_space=pltpu.HBM)
    return pl.pallas_call(
        functools.partial(correlate_kernel, places, arrays, part, norm),
        grid_spec=pltpu.PrefetchScalarGridSpec(
            num_scalar_prefetch=1,
            grid=(1,),
            in_specs=[any_spec] * len(operands),
            out_specs=any_spec,
            scratch_shapes=[
                pltpu.VMEM((count, days, rows, SAMPLES), BF),
                pltpu.VMEM((slots, count, days, BW, SAMPLES), BF),
                pltpu.VMEM((slots,) + tile[1:], jnp.float32),
                pltpu.VMEM(tile[1:] if first else (slots,) + tile[1:], jnp.float32),
            ]
            + [pltpu.VMEM((rows, span), BF)] * count
            + [pltpu.VMEM((2 * BW, span), BF)] * count
            + [pltpu.VMEM((GROUP * rows, span), BF)] * (GROUPS * count if slots > 1 else 2)
            + [pltpu.VMEM(tile[1:], jnp.float32)] * (count - 1)
            + [
                pltpu.SemaphoreType.DMA((count,)),
                pltpu.SemaphoreType.DMA((slots, count)),
                pltpu.SemaphoreType.DMA((TILES_DEV,)),
                pltpu.SemaphoreType.DMA((TILES_DEV,)),
            ],
        ),
        out_shape=jax.ShapeDtypeStruct(tile, jnp.float32),
        input_output_aliases=aliases,
        compiler_params=pltpu.CompilerParams(vmem_limit_bytes=(46 if slots * count > 3 else 32) << 20),
        cost_estimate=pl.CostEstimate(
            flops=1 << 20, bytes_accessed=1 << 16, transcendentals=0
        ),
        name=name,
    )(scalars, *operands)


def moved(array, axis, by):
    devices = lax.axis_size(axis)
    if axis == "day":
        pairs = [(i, (i + by) % devices) for i in range(devices)]
    else:
        pairs = [(i, i + by) for i in range(devices) if 0 <= i + by < devices]
    return lax.ppermute(array, axis, pairs)


def swapped(array):
    devices = lax.axis_size("chan")
    return lax.ppermute(array, "chan", [(i, i ^ 1) for i in range(devices)])


def local(strain_raw, pair_dist):
    day = lax.axis_index("day")
    even = lax.axis_index("chan") % 2 == 0
    rows = BW // lax.axis_size("day")
    total_days = strain_raw.shape[0] * lax.axis_size("day")
    norm = float((SAMPLES * total_days) ** -0.5)
    scalars = jnp.concatenate([day.astype(jnp.int32)[None], pair_dist[0].astype(jnp.int32)])

    own = whiten(strain_raw)
    tie = lax.optimization_barrier
    parity = (lax.axis_index("chan") % 2).astype(jnp.int32)[None]

    own_p, own_m, own_2 = (moved(own, "day", by) for by in (1, -1, 2))
    z2, z4 = moved(own, "chan", -2), moved(own, "chan", -4)
    own_p, own_m, own_2, z2, z4 = tie((own_p, own_m, own_2, z2, z4))

    z2_2, z4_2 = moved(own_2, "chan", -2), moved(own_2, "chan", -4)
    both = [(1, 0, 0, 0, 2), (2, 0, 0, 2, 2)]
    zz, mine = gather(
        parity,
        (own, z2, z4),
        (4, 4),
        both + [(1, 0, 1, 0, 2), (2, 0, 1, 2, 2)],
        both + [(0, 0, 1, 0, 2), (1, 0, 1, 2, 2)],
        "pair_near",
    )
    zz_p, zz_m = moved(zz, "day", 1), moved(zz, "day", -1)
    pair = swapped(mine)
    near = ((own, 0), {0: (own, 0), 1: (pair, 0), 2: (z2, 0), 3: (pair, 2), 4: (z4, 0)})
    tiles = correlate([near], "all", 3, scalars, None, rows, norm, "near_days")
    zz_p, zz_m, z2_2, z4_2, tiles = tie((zz_p, zz_m, z2_2, z4_2, tiles))

    (mine,) = gather(
        parity,
        (own_p, own_m, own_2, zz_p, zz_m, z2_2, z4_2),
        (12,),
        [(3, 0, 0, 0, 4), (4, 0, 0, 4, 4), (5, 0, 0, 8, 2), (6, 0, 0, 10, 2)],
        [
            (0, 0, 0, 0, 2),
            (3, 0, 0, 2, 2),
            (1, 0, 0, 4, 2),
            (4, 0, 0, 6, 2),
            (2, 0, 0, 8, 2),
            (5, 0, 0, 10, 2),
        ],
        "pair_far",
    )
    pair = swapped(mine)
    owns = (own_p, own_m, own_2)
    twos = ((zz_p, 0), (zz_m, 0), (z2_2, 0))
    fours = ((zz_p, 2), (zz_m, 2), (z4_2, 0))
    sets = [((owns[i], 0), {0: (owns[i], 0), 2: twos[i], 4: fours[i]}) for i in range(3)]
    tiles = correlate(sets, "head", 1, scalars, tiles, rows, norm, "far_days_one")
    sets = [
        (own, {**blocks, 1: (pair, 4 * i), 3: (pair, 4 * i + 2)})
        for i, (own, blocks) in enumerate(sets)
    ]
    return correlate(sets, "rest", 2, scalars, tiles, rows, norm, "far_days_rest")


def solution(mesh):
    placed = (P("day", "chan", None), P("chan", None))
    return jax.shard_map(
        local, mesh=mesh, in_specs=placed, out_specs=P("chan", None, "day", None), check_vma=False
    )
```

```python
import functools
import jax
import jax.numpy as jnp
from jax import lax
from jax.experimental import pallas as pl
from jax.experimental.pallas import tpu as pltpu
from jax.sharding import PartitionSpec as P

BW = 128
SAMPLES = 1024
MAXLAG = 64
REACH = 4
TILES_DEV = 3
LAGS = 2 * MAXLAG + 1
SHIFTS = MAXLAG + 1
GROUP = 13
GROUPS = SHIFTS // GROUP
BF = jnp.bfloat16


def whiten_kernel(raw_ref, out_ref):
    values = raw_ref[...].astype(jnp.float32)
    centred = values - jnp.mean(values, axis=-1, keepdims=True)
    spread = jnp.mean(centred * centred, axis=-1, keepdims=True)
    out_ref[...] = (centred * lax.rsqrt(spread + 1e-06)).astype(BF)


def whiten(strain_raw):
    return pl.pallas_call(
        whiten_kernel,
        in_specs=[pl.BlockSpec(memory_space=pltpu.VMEM)],
        out_specs=pl.BlockSpec(memory_space=pltpu.VMEM),
        out_shape=jax.ShapeDtypeStruct(strain_raw.shape, BF),
        cost_estimate=pl.CostEstimate(
            flops=8 * strain_raw.size, bytes_accessed=4 * strain_raw.size, transcendentals=0
        ),
        name="whiten",
    )(strain_raw)


def gather_kernel(moves, flag, *refs):
    arrays, outs, sems = refs[: moves[0]], refs[moves[0] : -1], refs[-1]
    for parity in (0, 1):

        @pl.when(flag[0] == parity)
        def _():
            copies = [
                pltpu.make_async_copy(
                    arrays[i].at[pl.ds(at, n)], outs[j].at[pl.ds(to, n)], sems.at[c]
                )
                for c, (i, at, j, to, n) in enumerate(moves[1 + parity])
            ]
            for copy in copies:
                copy.start()
            for copy in copies:
                copy.wait()


def gather(flag, arrays, counts, even, odd, name):
    vmem_spec = pl.BlockSpec(memory_space=pltpu.VMEM)
    any_spec = pl.BlockSpec(memory_space=pl.ANY)
    shape = arrays[0].shape[1:]
    return pl.pallas_call(
        functools.partial(gather_kernel, (len(arrays), even, odd)),
        in_specs=[pl.BlockSpec(memory_space=pltpu.SMEM)] + [any_spec] * len(arrays),
        out_specs=[vmem_spec] * len(counts),
        out_shape=[jax.ShapeDtypeStruct((n,) + shape, BF) for n in counts],
        scratch_shapes=[pltpu.SemaphoreType.DMA((max(len(even), len(odd)),))],
        compiler_params=pltpu.CompilerParams(vmem_limit_bytes=16 << 20),
        name=name,
    )(flag, *arrays)


def correlate_kernel(places, operands, part, norm, win, *refs):
    sets = len(places)
    first = part == "all"
    arrays, refs = refs[:operands], refs[operands:]
    if not first:
        refs = refs[1:]
    out_ref, araw, braw, tiles, before, *refs = refs
    lefts, rights, refs = refs[:sets], refs[sets : 2 * sets], refs[2 * sets :]
    shifted, sums, sems = refs[: 1 - sets - 4], refs[1 - sets - 4 : -4], refs[-4:]
    sem_a, sem_b, sem_in, sem_out = sems
    days, rows = araw.shape[1:3]
    slots = tiles.shape[0]
    row0 = pl.multiple_of(win[0] * rows, rows)

    lives, found = [], jnp.bool_(False)
    for k in range(TILES_DEV):
        dist = win[1 + k]
        plain = jnp.logical_and(dist >= 0, dist % 2 == 0)
        head = jnp.logical_and(plain, jnp.logical_not(found))
        found = jnp.logical_or(found, plain)
        if part == "all":
            lives.append(dist >= 0)
        elif part == "head":
            lives.append(head)
        else:
            lives.append(jnp.logical_and(dist >= 0, jnp.logical_not(head)))
    seats = [jnp.int32(0)]
    for k in range(TILES_DEV):
        seats.append(seats[-1] + lives[k].astype(jnp.int32))

    def copy_in(k, seat):
        return pltpu.make_async_copy(out_ref.at[k], before.at[seat], sem_in.at[seat])

    def copy_out(k, seat):
        return pltpu.make_async_copy(tiles.at[seat], out_ref.at[k], sem_out.at[seat])

    def copy_zero(k):
        return pltpu.make_async_copy(before, out_ref.at[k], sem_in.at[k])

    def copy_left(s):
        array, start = places[s][0]
        return pltpu.make_async_copy(
            arrays[array].at[pl.ds(start, days), pl.ds(row0, rows), :], araw.at[s], sem_a.at[s]
        )

    def copy_right(s, seat, n):
        array, start = places[s][1 + n]
        return pltpu.make_async_copy(
            arrays[array].at[pl.ds(start, days)], braw.at[seat, s], sem_b.at[seat, s]
        )

    @pl.when(seats[-1] > 0)
    def _():
        for s in range(sets):
            copy_left(s).start()
        for k in range(TILES_DEV):
            for e in range(0, REACH + 1, 2 if part == "head" else 1):

                @pl.when(jnp.logical_and(lives[k], win[1 + k] == e))
                def _():
                    for s in range(sets):
                        copy_right(s, seats[k], e).start()

            if not first:

                @pl.when(lives[k])
                def _():
                    copy_in(k, seats[k]).start()

        if first:
            before[...] = jnp.zeros(before.shape, jnp.float32)
            for k in range(TILES_DEV):
                pl.when(jnp.logical_not(lives[k]))(copy_zero(k).start)

        gap = jnp.zeros((rows, MAXLAG), BF)
        gap_b = jnp.zeros((BW, MAXLAG), BF)
        for s in range(sets):
            copy_left(s).wait()
            lefts[s][...] = jnp.concatenate(
                [p for d in range(days) for p in (araw[s, d], gap)], 1
            )

        def make_shift(s, g):
            for i in range(GROUP):
                shift = g * GROUP + i
                value = lefts[s][...]
                if shift:
                    value = pltpu.roll(value, shift, 1)
                shifted[(s * GROUPS + g) % len(shifted)][i * rows : (i + 1) * rows, :] = value

        def make_right(s, seat):
            rights[s][0:BW, :] = jnp.concatenate(
                [p for d in range(days) for p in (gap_b, braw[seat, s, d])], 1
            )
            rights[s][BW : 2 * BW, :] = jnp.concatenate(
                [p for d in range(days) for p in (braw[seat, s, d], gap_b)], 1
            )

        def work(seat, with_shift):
            for s in range(sets):
                copy_right(s, seat, 0).wait()
                make_right(s, seat)
            if not first:
                copy_in(0, seat).wait()
            if with_shift:
                make_shift(0, 0)
            for n in range(sets * GROUPS):
                s, g = divmod(n, GROUPS)
                if with_shift and n + 1 < sets * GROUPS:
                    make_shift(*divmod(n + 1, GROUPS))
                product = lax.dot_general(
                    shifted[n % len(shifted)][...],
                    rights[s][...],
                    (((1,), (1,)), ((), ())),
                    preferred_element_type=jnp.float32,
                )
                kept = GROUP - (g == GROUPS - 1)
                for half, count, lag in (
                    (0, kept, g * GROUP),
                    (1, GROUP, MAXLAG + g * GROUP),
                ):
                    value = product[:, half * BW : (half + 1) * BW]
                    value = value.reshape(GROUP, rows, BW)[:count]
                    at = pl.ds(lag, count)
                    if s:
                        value = value + sums[s - 1][at]
                    if s + 1 < sets:
                        sums[s][at] = value
                    elif first:
                        tiles[seat, at] = value * norm
                    else:
                        tiles[seat, at] = value * norm + before[seat, at]

        def loop(seat, carry):
            pl.when(seat == 0)(functools.partial(work, seat, True))
            if slots > 1:
                pl.when(seat > 0)(functools.partial(work, seat, False))
            for k in range(TILES_DEV):
                mine = jnp.logical_and(lives[k], seats[k] == seat)
                pl.when(mine)(copy_out(k, seat).start)
            return carry

        lax.fori_loop(0, seats[-1], loop, 0)

    for k in range(TILES_DEV):
        pl.when(lives[k])(copy_out(k, seats[k]).wait)
        if first:
            pl.when(jnp.logical_not(lives[k]))(copy_zero(k).wait)


def correlate(sets, part, slots, scalars, total, rows, norm, name):
    count = len(sets)
    days = 2
    span = days * (SAMPLES + MAXLAG)
    operands = []

    def place(block):
        array, start = block
        for i, other in enumerate(operands):
            if other is array:
                return i, start
        operands.append(array)
        return len(operands) - 1, start

    places = [
        [place(own)] + [place(partners.get(e, own)) for e in range(REACH + 1)] for own, partners in sets
    ]
    arrays = len(operands)
    first = part == "all"
    aliases = {}
    if not first:
        aliases = {1 + len(operands): 0}
        operands.append(total)
    tile = (TILES_DEV, LAGS, rows, BW)
    any_spec = pl.BlockSpec(memory_space=pltpu.HBM)
    return pl.pallas_call(
        functools.partial(correlate_kernel, places, arrays, part, norm),
        grid_spec=pltpu.PrefetchScalarGridSpec(
            num_scalar_prefetch=1,
            grid=(1,),
            in_specs=[any_spec] * len(operands),
            out_specs=any_spec,
            scratch_shapes=[
                pltpu.VMEM((count, days, rows, SAMPLES), BF),
                pltpu.VMEM((slots, count, days, BW, SAMPLES), BF),
                pltpu.VMEM((slots,) + tile[1:], jnp.float32),
                pltpu.VMEM(tile[1:] if first else (slots,) + tile[1:], jnp.float32),
            ]
            + [pltpu.VMEM((rows, span), BF)] * count
            + [pltpu.VMEM((2 * BW, span), BF)] * count
            + [pltpu.VMEM((GROUP * rows, span), BF)] * (GROUPS * count if slots > 1 else 2)
            + [pltpu.VMEM(tile[1:], jnp.float32)] * (count - 1)
            + [
                pltpu.SemaphoreType.DMA((count,)),
                pltpu.SemaphoreType.DMA((slots, count)),
                pltpu.SemaphoreType.DMA((TILES_DEV,)),
                pltpu.SemaphoreType.DMA((TILES_DEV,)),
            ],
        ),
        out_shape=jax.ShapeDtypeStruct(tile, jnp.float32),
        input_output_aliases=aliases,
        compiler_params=pltpu.CompilerParams(vmem_limit_bytes=(46 if slots * count > 3 else 32) << 20),
        cost_estimate=pl.CostEstimate(
            flops=1 << 20, bytes_accessed=1 << 16, transcendentals=0
        ),
        name=name,
    )(scalars, *operands)


def moved(array, axis, by):
    devices = lax.axis_size(axis)
    if axis == "day":
        pairs = [(i, (i + by) % devices) for i in range(devices)]
    else:
        pairs = [(i, i + by) for i in range(devices) if 0 <= i + by < devices]
    return lax.ppermute(array, axis, pairs)


def swapped(array):
    devices = lax.axis_size("chan")
    return lax.ppermute(array, "chan", [(i, i ^ 1) for i in range(devices)])


def local(strain_raw, pair_dist):
    day = lax.axis_index("day")
    even = lax.axis_index("chan") % 2 == 0
    rows = BW // lax.axis_size("day")
    total_days = strain_raw.shape[0] * lax.axis_size("day")
    norm = float((SAMPLES * total_days) ** -0.5)
    scalars = jnp.concatenate([day.astype(jnp.int32)[None], pair_dist[0].astype(jnp.int32)])

    own = whiten(strain_raw)
    tie = lax.optimization_barrier
    parity = (lax.axis_index("chan") % 2).astype(jnp.int32)[None]

    own_2, z2 = moved(own, "day", 2), moved(own, "chan", -2)
    own_m, own_p = moved(own, "day", -1), moved(own, "day", 1)
    z4 = moved(own, "chan", -4)
    own_2, z2, own_m, own_p, z4 = tie((own_2, z2, own_m, own_p, z4))

    z2_2, z4_2 = moved(own_2, "chan", -2), moved(own_2, "chan", -4)
    both = [(1, 0, 0, 0, 2), (2, 0, 0, 2, 2)]
    zz, mine = gather(
        parity,
        (own, z2, z4),
        (4, 4),
        both + [(1, 0, 1, 0, 2), (2, 0, 1, 2, 2)],
        both + [(0, 0, 1, 0, 2), (1, 0, 1, 2, 2)],
        "pair_near",
    )
    zz_p, zz_m = moved(zz, "day", 1), moved(zz, "day", -1)
    pair = swapped(mine)
    near = ((own, 0), {0: (own, 0), 1: (pair, 0), 2: (z2, 0), 3: (pair, 2), 4: (z4, 0)})
    tiles = correlate([near], "all", 3, scalars, None, rows, norm, "near_days")
    zz_p, zz_m, z2_2, z4_2, tiles = tie((zz_p, zz_m, z2_2, z4_2, tiles))

    (mine,) = gather(
        parity,
        (own_p, own_m, own_2, zz_p, zz_m, z2_2, z4_2),
        (12,),
        [(3, 0, 0, 0, 4), (4, 0, 0, 4, 4), (5, 0, 0, 8, 2), (6, 0, 0, 10, 2)],
        [
            (0, 0, 0, 0, 2),
            (3, 0, 0, 2, 2),
            (1, 0, 0, 4, 2),
            (4, 0, 0, 6, 2),
            (2, 0, 0, 8, 2),
            (5, 0, 0, 10, 2),
        ],
        "pair_far",
    )
    pair = swapped(mine)
    owns = (own_p, own_m, own_2)
    twos = ((zz_p, 0), (zz_m, 0), (z2_2, 0))
    fours = ((zz_p, 2), (zz_m, 2), (z4_2, 0))
    sets = [((owns[i], 0), {0: (owns[i], 0), 2: twos[i], 4: fours[i]}) for i in range(3)]
    tiles = correlate(sets, "head", 1, scalars, tiles, rows, norm, "far_days_one")
    sets = [
        (own, {**blocks, 1: (pair, 4 * i), 3: (pair, 4 * i + 2)})
        for i, (own, blocks) in enumerate(sets)
    ]
    return correlate(sets, "rest", 2, scalars, tiles, rows, norm, "far_days_rest")


def solution(mesh):
    placed = (P("day", "chan", None), P("chan", None))
    return jax.shard_map(
        local, mesh=mesh, in_specs=placed, out_specs=P("chan", None, "day", None), check_vma=False
    )
```

```python
import functools
import jax
import jax.numpy as jnp
from jax import lax
from jax.experimental import pallas as pl
from jax.experimental.pallas import tpu as pltpu
from jax.sharding import PartitionSpec as P

BW = 128
SAMPLES = 1024
MAXLAG = 64
REACH = 4
TILES_DEV = 3
LAGS = 2 * MAXLAG + 1
SHIFTS = MAXLAG + 1
GROUP = 13
GROUPS = SHIFTS // GROUP
BF = jnp.bfloat16


def whiten_kernel(raw_ref, out_ref):
    values = raw_ref[...].astype(jnp.float32)
    centred = values - jnp.mean(values, axis=-1, keepdims=True)
    spread = jnp.mean(centred * centred, axis=-1, keepdims=True)
    out_ref[...] = (centred * lax.rsqrt(spread + 1e-06)).astype(BF)


def whiten(strain_raw):
    return pl.pallas_call(
        whiten_kernel,
        in_specs=[pl.BlockSpec(memory_space=pltpu.VMEM)],
        out_specs=pl.BlockSpec(memory_space=pltpu.VMEM),
        out_shape=jax.ShapeDtypeStruct(strain_raw.shape, BF),
        cost_estimate=pl.CostEstimate(
            flops=8 * strain_raw.size, bytes_accessed=4 * strain_raw.size, transcendentals=0
        ),
        name="whiten",
    )(strain_raw)


def gather_kernel(moves, flag, *refs):
    arrays, outs, sems = refs[: moves[0]], refs[moves[0] : -1], refs[-1]
    for parity in (0, 1):

        @pl.when(flag[0] == parity)
        def _():
            copies = [
                pltpu.make_async_copy(
                    arrays[i].at[pl.ds(at, n)], outs[j].at[pl.ds(to, n)], sems.at[c]
                )
                for c, (i, at, j, to, n) in enumerate(moves[1 + parity])
            ]
            for copy in copies:
                copy.start()
            for copy in copies:
                copy.wait()


def gather(flag, arrays, counts, even, odd, name):
    vmem_spec = pl.BlockSpec(memory_space=pltpu.VMEM)
    any_spec = pl.BlockSpec(memory_space=pl.ANY)
    shape = arrays[0].shape[1:]
    return pl.pallas_call(
        functools.partial(gather_kernel, (len(arrays), even, odd)),
        in_specs=[pl.BlockSpec(memory_space=pltpu.SMEM)] + [any_spec] * len(arrays),
        out_specs=[vmem_spec] * len(counts),
        out_shape=[jax.ShapeDtypeStruct((n,) + shape, BF) for n in counts],
        scratch_shapes=[pltpu.SemaphoreType.DMA((max(len(even), len(odd)),))],
        compiler_params=pltpu.CompilerParams(vmem_limit_bytes=16 << 20),
        name=name,
    )(flag, *arrays)


def correlate_kernel(places, operands, part, norm, win, *refs):
    sets = len(places)
    first = part == "all"
    arrays, refs = refs[:operands], refs[operands:]
    if not first:
        refs = refs[1:]
    out_ref, araw, braw, tiles, before, *refs = refs
    lefts, rights, refs = refs[:sets], refs[sets : 2 * sets], refs[2 * sets :]
    shifted, sums, sems = refs[: 1 - sets - 4], refs[1 - sets - 4 : -4], refs[-4:]
    sem_a, sem_b, sem_in, sem_out = sems
    days, rows = araw.shape[1:3]
    slots = tiles.shape[0]
    row0 = pl.multiple_of(win[0] * rows, rows)

    lives, found = [], jnp.bool_(False)
    for k in range(TILES_DEV):
        dist = win[1 + k]
        plain = jnp.logical_and(dist >= 0, dist % 2 == 0)
        head = jnp.logical_and(plain, jnp.logical_not(found))
        found = jnp.logical_or(found, plain)
        if part == "all":
            lives.append(dist >= 0)
        elif part == "head":
            lives.append(head)
        else:
            lives.append(jnp.logical_and(dist >= 0, jnp.logical_not(head)))
    seats = [jnp.int32(0)]
    for k in range(TILES_DEV):
        seats.append(seats[-1] + lives[k].astype(jnp.int32))

    def copy_in(k, seat):
        return pltpu.make_async_copy(out_ref.at[k], before.at[seat], sem_in.at[seat])

    def copy_out(k, seat):
        return pltpu.make_async_copy(tiles.at[seat], out_ref.at[k], sem_out.at[seat])

    def copy_lags(k, seat, at, to):
        lags = pl.ds(at, to - at)
        return pltpu.make_async_copy(
            tiles.at[seat, lags], out_ref.at[k, lags], sem_out.at[seat]
        )

    def copy_zero(k):
        return pltpu.make_async_copy(before, out_ref.at[k], sem_in.at[k])

    def copy_left(s):
        array, start = places[s][0]
        return pltpu.make_async_copy(
            arrays[array].at[pl.ds(start, days), pl.ds(row0, rows), :], araw.at[s], sem_a.at[s]
        )

    def copy_right(s, seat, n):
        array, start = places[s][1 + n]
        return pltpu.make_async_copy(
            arrays[array].at[pl.ds(start, days)], braw.at[seat, s], sem_b.at[seat, s]
        )

    @pl.when(seats[-1] > 0)
    def _():
        for s in range(sets):
            copy_left(s).start()
            for k in range(TILES_DEV):
                for e in range(0, REACH + 1, 2 if part == "head" else 1):

                    @pl.when(jnp.logical_and(lives[k], win[1 + k] == e))
                    def _():
                        copy_right(s, seats[k], e).start()

        if not first:
            for k in range(TILES_DEV):

                @pl.when(lives[k])
                def _():
                    copy_in(k, seats[k]).start()

        if first:
            before[...] = jnp.zeros(before.shape, jnp.float32)
            for k in range(TILES_DEV):
                pl.when(jnp.logical_not(lives[k]))(copy_zero(k).start)

        gap = jnp.zeros((rows, MAXLAG), BF)
        gap_b = jnp.zeros((BW, MAXLAG), BF)
        for s in range(sets):
            copy_left(s).wait()
            lefts[s][...] = jnp.concatenate(
                [p for d in range(days) for p in (araw[s, d], gap)], 1
            )

        def make_shift(s, g):
            for i in range(GROUP):
                shift = g * GROUP + i
                value = lefts[s][...]
                if shift:
                    value = pltpu.roll(value, shift, 1)
                shifted[(s * GROUPS + g) % len(shifted)][i * rows : (i + 1) * rows, :] = value

        def make_right(s, seat):
            rights[s][0:BW, :] = jnp.concatenate(
                [p for d in range(days) for p in (gap_b, braw[seat, s, d])], 1
            )
            rights[s][BW : 2 * BW, :] = jnp.concatenate(
                [p for d in range(days) for p in (braw[seat, s, d], gap_b)], 1
            )

        def work(k, seat, with_shift):
            late = part == "head"
            for s in range(1 if late else sets):
                copy_right(s, seat, 0).wait()
            if not first and not late:
                copy_in(0, seat).wait()
            make_right(0, seat)
            if with_shift:
                make_shift(0, 0)
            for n in range(sets * GROUPS):
                s, g = divmod(n, GROUPS)
                if late and n == 1:
                    for r in range(1, sets):
                        copy_right(r, seat, 0).wait()
                if g == 1 and s + 1 < sets:
                    make_right(s + 1, seat)
                if late and n == (sets - 1) * GROUPS:
                    copy_in(0, seat).wait()
                if with_shift and n + 1 < sets * GROUPS:
                    make_shift(*divmod(n + 1, GROUPS))
                product = lax.dot_general(
                    shifted[n % len(shifted)][...],
                    rights[s][...],
                    (((1,), (1,)), ((), ())),
                    preferred_element_type=jnp.float32,
                )
                kept = GROUP - (g == GROUPS - 1)
                for half, count, lag in (
                    (0, kept, g * GROUP),
                    (1, GROUP, MAXLAG + g * GROUP),
                ):
                    value = product[:, half * BW : (half + 1) * BW]
                    value = value.reshape(GROUP, rows, BW)[:count]
                    at = pl.ds(lag, count)
                    if s:
                        value = value + sums[s - 1][at]
                    if s + 1 < sets:
                        sums[s][at] = value
                    elif first:
                        tiles[seat, at] = value * norm
                    else:
                        tiles[seat, at] = value * norm + before[seat, at]
                if s + 1 == sets and g >= GROUPS - 2:
                    at, to = (0, g * GROUP + GROUP) if g < GROUPS - 1 else (g * GROUP, MAXLAG)
                    copy_lags(k, seat, at, to).start()
                    copy_lags(k, seat, MAXLAG + at, LAGS if to == MAXLAG else MAXLAG + to).start()

        def loop(seat, carry):
            k = jnp.int32(0)
            for n in range(TILES_DEV):
                k = jnp.where(jnp.logical_and(lives[n], seats[n] == seat), n, k)
            pl.when(seat == 0)(functools.partial(work, k, seat, True))
            if slots > 1:
                pl.when(seat > 0)(functools.partial(work, k, seat, False))
            return carry

        lax.fori_loop(0, seats[-1], loop, 0)

    for k in range(TILES_DEV):
        pl.when(lives[k])(copy_out(k, seats[k]).wait)
        if first:
            pl.when(jnp.logical_not(lives[k]))(copy_zero(k).wait)


def correlate(sets, part, slots, scalars, total, rows, norm, name):
    count = len(sets)
    days = 2
    span = days * (SAMPLES + MAXLAG)
    operands = []

    def place(block):
        array, start = block
        for i, other in enumerate(operands):
            if other is array:
                return i, start
        operands.append(array)
        return len(operands) - 1, start

    places = [
        [place(own)] + [place(partners.get(e, own)) for e in range(REACH + 1)] for own, partners in sets
    ]
    arrays = len(operands)
    first = part == "all"
    aliases = {}
    if not first:
        aliases = {1 + len(operands): 0}
        operands.append(total)
    tile = (TILES_DEV, LAGS, rows, BW)
    any_spec = pl.BlockSpec(memory_space=pltpu.HBM)
    return pl.pallas_call(
        functools.partial(correlate_kernel, places, arrays, part, norm),
        grid_spec=pltpu.PrefetchScalarGridSpec(
            num_scalar_prefetch=1,
            grid=(1,),
            in_specs=[any_spec] * len(operands),
            out_specs=any_spec,
            scratch_shapes=[
                pltpu.VMEM((count, days, rows, SAMPLES), BF),
                pltpu.VMEM((slots, count, days, BW, SAMPLES), BF),
                pltpu.VMEM((slots,) + tile[1:], jnp.float32),
                pltpu.VMEM(tile[1:] if first else (slots,) + tile[1:], jnp.float32),
            ]
            + [pltpu.VMEM((rows, span), BF)] * count
            + [pltpu.VMEM((2 * BW, span), BF)] * count
            + [pltpu.VMEM((GROUP * rows, span), BF)] * (GROUPS * count if slots > 1 else 2)
            + [pltpu.VMEM(tile[1:], jnp.float32)] * (count - 1)
            + [
                pltpu.SemaphoreType.DMA((count,)),
                pltpu.SemaphoreType.DMA((slots, count)),
                pltpu.SemaphoreType.DMA((TILES_DEV,)),
                pltpu.SemaphoreType.DMA((TILES_DEV,)),
            ],
        ),
        out_shape=jax.ShapeDtypeStruct(tile, jnp.float32),
        input_output_aliases=aliases,
        compiler_params=pltpu.CompilerParams(vmem_limit_bytes=(46 if slots * count > 3 else 32) << 20),
        cost_estimate=pl.CostEstimate(
            flops=1 << 20, bytes_accessed=1 << 16, transcendentals=0
        ),
        name=name,
    )(scalars, *operands)


def moved(array, axis, by):
    devices = lax.axis_size(axis)
    if axis == "day":
        pairs = [(i, (i + by) % devices) for i in range(devices)]
    else:
        pairs = [(i, i + by) for i in range(devices) if 0 <= i + by < devices]
    return lax.ppermute(array, axis, pairs)


def swapped(array):
    devices = lax.axis_size("chan")
    return lax.ppermute(array, "chan", [(i, i ^ 1) for i in range(devices)])


def local(strain_raw, pair_dist):
    day = lax.axis_index("day")
    even = lax.axis_index("chan") % 2 == 0
    rows = BW // lax.axis_size("day")
    total_days = strain_raw.shape[0] * lax.axis_size("day")
    norm = float((SAMPLES * total_days) ** -0.5)
    scalars = jnp.concatenate([day.astype(jnp.int32)[None], pair_dist[0].astype(jnp.int32)])

    own = whiten(strain_raw)
    tie = lax.optimization_barrier
    parity = (lax.axis_index("chan") % 2).astype(jnp.int32)[None]

    own_2, z2 = moved(own, "day", 2), moved(own, "chan", -2)
    own_m, own_p = moved(own, "day", -1), moved(own, "day", 1)
    z4 = moved(own, "chan", -4)
    own_2, z2, own_m, own_p, z4 = tie((own_2, z2, own_m, own_p, z4))

    z2_2, z4_2 = moved(own_2, "chan", -2), moved(own_2, "chan", -4)
    both = [(1, 0, 0, 0, 2), (2, 0, 0, 2, 2)]
    zz, mine = gather(
        parity,
        (own, z2, z4),
        (4, 4),
        both + [(1, 0, 1, 0, 2), (2, 0, 1, 2, 2)],
        both + [(0, 0, 1, 0, 2), (1, 0, 1, 2, 2)],
        "pair_near",
    )
    zz_p, zz_m = moved(zz, "day", 1), moved(zz, "day", -1)
    pair = swapped(mine)
    near = ((own, 0), {0: (own, 0), 1: (pair, 0), 2: (z2, 0), 3: (pair, 2), 4: (z4, 0)})
    tiles = correlate([near], "all", 3, scalars, None, rows, norm, "near_days")
    zz_p, zz_m, z2_2, z4_2, tiles = tie((zz_p, zz_m, z2_2, z4_2, tiles))

    (mine,) = gather(
        parity,
        (own_p, own_m, own_2, zz_p, zz_m, z2_2, z4_2),
        (12,),
        [(3, 0, 0, 0, 4), (4, 0, 0, 4, 4), (5, 0, 0, 8, 2), (6, 0, 0, 10, 2)],
        [
            (0, 0, 0, 0, 2),
            (3, 0, 0, 2, 2),
            (1, 0, 0, 4, 2),
            (4, 0, 0, 6, 2),
            (2, 0, 0, 8, 2),
            (5, 0, 0, 10, 2),
        ],
        "pair_far",
    )
    pair = swapped(mine)
    owns = (own_p, own_m, own_2)
    twos = ((zz_p, 0), (zz_m, 0), (z2_2, 0))
    fours = ((zz_p, 2), (zz_m, 2), (z4_2, 0))
    sets = [((owns[i], 0), {0: (owns[i], 0), 2: twos[i], 4: fours[i]}) for i in range(3)]
    tiles = correlate(sets, "head", 1, scalars, tiles, rows, norm, "far_days_one")
    sets = [
        (own, {**blocks, 1: (pair, 4 * i), 3: (pair, 4 * i + 2)})
        for i, (own, blocks) in enumerate(sets)
    ]
    return correlate(sets, "rest", 2, scalars, tiles, rows, norm, "far_days_rest")


def solution(mesh):
    placed = (P("day", "chan", None), P("chan", None))
    return jax.shard_map(
        local, mesh=mesh, in_specs=placed, out_specs=P("chan", None, "day", None), check_vma=False
    )
```

```python
import functools
import jax
import jax.numpy as jnp
from jax import lax
from jax.experimental import pallas as pl
from jax.experimental.pallas import tpu as pltpu
from jax.sharding import PartitionSpec as P

BW = 128
SAMPLES = 1024
MAXLAG = 64
REACH = 4
TILES_DEV = 3
LAGS = 2 * MAXLAG + 1
SHIFTS = MAXLAG + 1
GROUP = 13
GROUPS = SHIFTS // GROUP
BF = jnp.bfloat16


def whiten_kernel(raw_ref, out_ref):
    values = raw_ref[...].astype(jnp.float32)
    centred = values - jnp.mean(values, axis=-1, keepdims=True)
    spread = jnp.mean(centred * centred, axis=-1, keepdims=True)
    out_ref[...] = (centred * lax.rsqrt(spread + 1e-06)).astype(BF)


def whiten(strain_raw):
    return pl.pallas_call(
        whiten_kernel,
        in_specs=[pl.BlockSpec(memory_space=pltpu.VMEM)],
        out_specs=pl.BlockSpec(memory_space=pltpu.VMEM),
        out_shape=jax.ShapeDtypeStruct(strain_raw.shape, BF),
        cost_estimate=pl.CostEstimate(
            flops=8 * strain_raw.size, bytes_accessed=4 * strain_raw.size, transcendentals=0
        ),
        name="whiten",
    )(strain_raw)


def gather_kernel(moves, flag, *refs):
    arrays, outs, sems = refs[: moves[0]], refs[moves[0] : -1], refs[-1]
    for parity in (0, 1):

        @pl.when(flag[0] == parity)
        def _():
            copies = [
                pltpu.make_async_copy(
                    arrays[i].at[pl.ds(at, n)], outs[j].at[pl.ds(to, n)], sems.at[c]
                )
                for c, (i, at, j, to, n) in enumerate(moves[1 + parity])
            ]
            for copy in copies:
                copy.start()
            for copy in copies:
                copy.wait()


def gather(flag, arrays, counts, even, odd, name):
    vmem_spec = pl.BlockSpec(memory_space=pltpu.VMEM)
    any_spec = pl.BlockSpec(memory_space=pl.ANY)
    shape = arrays[0].shape[1:]
    return pl.pallas_call(
        functools.partial(gather_kernel, (len(arrays), even, odd)),
        in_specs=[pl.BlockSpec(memory_space=pltpu.SMEM)] + [any_spec] * len(arrays),
        out_specs=[vmem_spec] * len(counts),
        out_shape=[jax.ShapeDtypeStruct((n,) + shape, BF) for n in counts],
        scratch_shapes=[pltpu.SemaphoreType.DMA((max(len(even), len(odd)),))],
        compiler_params=pltpu.CompilerParams(vmem_limit_bytes=16 << 20),
        name=name,
    )(flag, *arrays)


def correlate_kernel(places, operands, part, norm, win, *refs):
    sets = len(places)
    first = part == "all"
    arrays, refs = refs[:operands], refs[operands:]
    if not first:
        refs = refs[1:]
    out_ref, araw, braw, tiles, before, *refs = refs
    lefts, rights, refs = refs[:sets], refs[sets : 2 * sets], refs[2 * sets :]
    shifted, sums, sems = refs[: 1 - sets - 4], refs[1 - sets - 4 : -4], refs[-4:]
    sem_a, sem_b, sem_in, sem_out = sems
    days, rows = araw.shape[1:3]
    slots = tiles.shape[0]
    row0 = pl.multiple_of(win[0] * rows, rows)

    lives, found = [], jnp.bool_(False)
    for k in range(TILES_DEV):
        dist = win[1 + k]
        plain = jnp.logical_and(dist >= 0, dist % 2 == 0)
        head = jnp.logical_and(plain, jnp.logical_not(found))
        found = jnp.logical_or(found, plain)
        if part == "all":
            lives.append(dist >= 0)
        elif part == "head":
            lives.append(head)
        else:
            lives.append(jnp.logical_and(dist >= 0, jnp.logical_not(head)))
    seats = [jnp.int32(0)]
    for k in range(TILES_DEV):
        seats.append(seats[-1] + lives[k].astype(jnp.int32))

    def copy_in(k, seat):
        return pltpu.make_async_copy(out_ref.at[k], before.at[seat], sem_in.at[seat])

    def copy_out(k, seat):
        return pltpu.make_async_copy(tiles.at[seat], out_ref.at[k], sem_out.at[seat])

    def copy_lags(k, seat, at, to):
        lags = pl.ds(at, to - at)
        return pltpu.make_async_copy(
            tiles.at[seat, lags], out_ref.at[k, lags], sem_out.at[seat]
        )

    def copy_zero(k):
        return pltpu.make_async_copy(before, out_ref.at[k], sem_in.at[k])

    def copy_left(s):
        array, start = places[s][0]
        return pltpu.make_async_copy(
            arrays[array].at[pl.ds(start, days), pl.ds(row0, rows), :], araw.at[s], sem_a.at[s]
        )

    def copy_right(s, seat, n):
        array, start = places[s][1 + n]
        return pltpu.make_async_copy(
            arrays[array].at[pl.ds(start, days)], braw.at[seat, s], sem_b.at[seat, s]
        )

    @pl.when(seats[-1] > 0)
    def _():
        for s in range(sets):
            copy_left(s).start()
            for k in range(TILES_DEV):
                for e in range(0, REACH + 1, 2 if part == "head" else 1):

                    @pl.when(jnp.logical_and(lives[k], win[1 + k] == e))
                    def _():
                        copy_right(s, seats[k], e).start()

        if not first:
            for k in range(TILES_DEV):

                @pl.when(lives[k])
                def _():
                    copy_in(k, seats[k]).start()

        if first:
            before[...] = jnp.zeros(before.shape, jnp.float32)
            for k in range(TILES_DEV):
                pl.when(jnp.logical_not(lives[k]))(copy_zero(k).start)

        gap = jnp.zeros((rows, 2 * MAXLAG), BF)
        gap_b = jnp.zeros((BW, MAXLAG), BF)
        for s in range(sets):
            copy_left(s).wait()
            lefts[s][...] = jnp.concatenate(
                [p for d in range(days) for p in (araw[s, d], gap)], 1
            )

        def make_shift(s, g):
            for i in range(GROUP):
                shift = g * GROUP + i
                value = lefts[s][...]
                if shift:
                    value = pltpu.roll(value, shift, 1)
                shifted[(s * GROUPS + g) % len(shifted)][i * rows : (i + 1) * rows, :] = value

        def make_right(s, seat):
            rights[s][0:BW, :] = jnp.concatenate(
                [p for d in range(days) for p in (gap_b, braw[seat, s, d], gap_b)], 1
            )
            rights[s][BW : 2 * BW, :] = jnp.concatenate(
                [p for d in range(days) for p in (braw[seat, s, d], gap_b, gap_b)], 1
            )

        def work(k, seat, with_shift):
            late = part == "head"
            for s in range(1 if late else sets):
                copy_right(s, seat, 0).wait()
            if not first and not late:
                copy_in(0, seat).wait()
            make_right(0, seat)
            if with_shift:
                make_shift(0, 0)
            for n in range(sets * GROUPS):
                s, g = divmod(n, GROUPS)
                if late and n == 1:
                    for r in range(1, sets):
                        copy_right(r, seat, 0).wait()
                if g == 1 and s + 1 < sets:
                    make_right(s + 1, seat)
                if late and n == (sets - 1) * GROUPS:
                    copy_in(0, seat).wait()
                if with_shift and n + 1 < sets * GROUPS:
                    make_shift(*divmod(n + 1, GROUPS))
                product = lax.dot_general(
                    shifted[n % len(shifted)][...],
                    rights[s][...],
                    (((1,), (1,)), ((), ())),
                    preferred_element_type=jnp.float32,
                )
                kept = GROUP - (g == GROUPS - 1)
                for half, count, lag in (
                    (0, kept, g * GROUP),
                    (1, GROUP, MAXLAG + g * GROUP),
                ):
                    value = product[:, half * BW : (half + 1) * BW]
                    value = value.reshape(GROUP, rows, BW)[:count]
                    at = pl.ds(lag, count)
                    if s:
                        value = value + sums[s - 1][at]
                    if s + 1 < sets:
                        sums[s][at] = value
                    elif first:
                        tiles[seat, at] = value * norm
                    else:
                        tiles[seat, at] = value * norm + before[seat, at]
                if s + 1 == sets and g >= GROUPS - 2:
                    at, to = (0, g * GROUP + GROUP) if g < GROUPS - 1 else (g * GROUP, MAXLAG)
                    copy_lags(k, seat, at, to).start()
                    copy_lags(k, seat, MAXLAG + at, LAGS if to == MAXLAG else MAXLAG + to).start()

        def loop(seat, carry):
            k = jnp.int32(0)
            for n in range(TILES_DEV):
                k = jnp.where(jnp.logical_and(lives[n], seats[n] == seat), n, k)
            pl.when(seat == 0)(functools.partial(work, k, seat, True))
            if slots > 1:
                pl.when(seat > 0)(functools.partial(work, k, seat, False))
            return carry

        lax.fori_loop(0, seats[-1], loop, 0)

    for k in range(TILES_DEV):
        pl.when(lives[k])(copy_out(k, seats[k]).wait)
        if first:
            pl.when(jnp.logical_not(lives[k]))(copy_zero(k).wait)


def correlate(sets, part, slots, scalars, total, rows, norm, name):
    count = len(sets)
    days = 2
    span = days * (SAMPLES + 2 * MAXLAG)
    operands = []

    def place(block):
        array, start = block
        for i, other in enumerate(operands):
            if other is array:
                return i, start
        operands.append(array)
        return len(operands) - 1, start

    places = [
        [place(own)] + [place(partners.get(e, own)) for e in range(REACH + 1)] for own, partners in sets
    ]
    arrays = len(operands)
    first = part == "all"
    aliases = {}
    if not first:
        aliases = {1 + len(operands): 0}
        operands.append(total)
    tile = (TILES_DEV, LAGS, rows, BW)
    any_spec = pl.BlockSpec(memory_space=pltpu.HBM)
    return pl.pallas_call(
        functools.partial(correlate_kernel, places, arrays, part, norm),
        grid_spec=pltpu.PrefetchScalarGridSpec(
            num_scalar_prefetch=1,
            grid=(1,),
            in_specs=[any_spec] * len(operands),
            out_specs=any_spec,
            scratch_shapes=[
                pltpu.VMEM((count, days, rows, SAMPLES), BF),
                pltpu.VMEM((slots, count, days, BW, SAMPLES), BF),
                pltpu.VMEM((slots,) + tile[1:], jnp.float32),
                pltpu.VMEM(tile[1:] if first else (slots,) + tile[1:], jnp.float32),
            ]
            + [pltpu.VMEM((rows, span), BF)] * count
            + [pltpu.VMEM((2 * BW, span), BF)] * count
            + [pltpu.VMEM((GROUP * rows, span), BF)] * (GROUPS * count if slots > 1 else 2)
            + [pltpu.VMEM(tile[1:], jnp.float32)] * (count - 1)
            + [
                pltpu.SemaphoreType.DMA((count,)),
                pltpu.SemaphoreType.DMA((slots, count)),
                pltpu.SemaphoreType.DMA((TILES_DEV,)),
                pltpu.SemaphoreType.DMA((TILES_DEV,)),
            ],
        ),
        out_shape=jax.ShapeDtypeStruct(tile, jnp.float32),
        input_output_aliases=aliases,
        compiler_params=pltpu.CompilerParams(vmem_limit_bytes=(48 if slots * count > 3 else 32) << 20),
        cost_estimate=pl.CostEstimate(
            flops=1 << 20, bytes_accessed=1 << 16, transcendentals=0
        ),
        name=name,
    )(scalars, *operands)


def moved(array, axis, by):
    devices = lax.axis_size(axis)
    if axis == "day":
        pairs = [(i, (i + by) % devices) for i in range(devices)]
    else:
        pairs = [(i, i + by) for i in range(devices) if 0 <= i + by < devices]
    return lax.ppermute(array, axis, pairs)


def swapped(array):
    devices = lax.axis_size("chan")
    return lax.ppermute(array, "chan", [(i, i ^ 1) for i in range(devices)])


def local(strain_raw, pair_dist):
    day = lax.axis_index("day")
    even = lax.axis_index("chan") % 2 == 0
    rows = BW // lax.axis_size("day")
    total_days = strain_raw.shape[0] * lax.axis_size("day")
    norm = float((SAMPLES * total_days) ** -0.5)
    scalars = jnp.concatenate([day.astype(jnp.int32)[None], pair_dist[0].astype(jnp.int32)])

    own = whiten(strain_raw)
    tie = lax.optimization_barrier
    parity = (lax.axis_index("chan") % 2).astype(jnp.int32)[None]

    own_2, z2 = moved(own, "day", 2), moved(own, "chan", -2)
    own_m, own_p = moved(own, "day", -1), moved(own, "day", 1)
    z4 = moved(own, "chan", -4)
    own_2, z2, own_m, own_p, z4 = tie((own_2, z2, own_m, own_p, z4))

    z2_2, z4_2 = moved(own_2, "chan", -2), moved(own_2, "chan", -4)
    both = [(1, 0, 0, 0, 2), (2, 0, 0, 2, 2)]
    zz, mine = gather(
        parity,
        (own, z2, z4),
        (4, 4),
        both + [(1, 0, 1, 0, 2), (2, 0, 1, 2, 2)],
        both + [(0, 0, 1, 0, 2), (1, 0, 1, 2, 2)],
        "pair_near",
    )
    zz_p, zz_m = moved(zz, "day", 1), moved(zz, "day", -1)
    pair = swapped(mine)
    near = ((own, 0), {0: (own, 0), 1: (pair, 0), 2: (z2, 0), 3: (pair, 2), 4: (z4, 0)})
    tiles = correlate([near], "all", 3, scalars, None, rows, norm, "near_days")
    zz_p, zz_m, z2_2, z4_2, tiles = tie((zz_p, zz_m, z2_2, z4_2, tiles))

    (mine,) = gather(
        parity,
        (own_p, own_m, own_2, zz_p, zz_m, z2_2, z4_2),
        (12,),
        [(3, 0, 0, 0, 4), (4, 0, 0, 4, 4), (5, 0, 0, 8, 2), (6, 0, 0, 10, 2)],
        [
            (0, 0, 0, 0, 2),
            (3, 0, 0, 2, 2),
            (1, 0, 0, 4, 2),
            (4, 0, 0, 6, 2),
            (2, 0, 0, 8, 2),
            (5, 0, 0, 10, 2),
        ],
        "pair_far",
    )
    pair = swapped(mine)
    owns = (own_p, own_m, own_2)
    twos = ((zz_p, 0), (zz_m, 0), (z2_2, 0))
    fours = ((zz_p, 2), (zz_m, 2), (z4_2, 0))
    sets = [((owns[i], 0), {0: (owns[i], 0), 2: twos[i], 4: fours[i]}) for i in range(3)]
    tiles = correlate(sets, "head", 1, scalars, tiles, rows, norm, "far_days_one")
    sets = [
        (own, {**blocks, 1: (pair, 4 * i), 3: (pair, 4 * i + 2)})
        for i, (own, blocks) in enumerate(sets)
    ]
    return correlate(sets, "rest", 2, scalars, tiles, rows, norm, "far_days_rest")


def solution(mesh):
    placed = (P("day", "chan", None), P("chan", None))
    return jax.shard_map(
        local, mesh=mesh, in_specs=placed, out_specs=P("chan", None, "day", None), check_vma=False
    )
```
